32 devices in a mesh: outer: 8 (over z, x), inner: 4 (over y, core).
Axes of the slice: x: 2, y: 2, z: 4, core: 2. Of those that a mesh axis runs over, the one named last changes fastest.
Arguments:
- queries: bfloat16 [4096, 1024], P(('outer', 'inner')), may hold values from -6 to 6
- keys: bfloat16 [4096, 1024], P(('outer', 'inner')), may hold values from -6 to 6
- values: bfloat16 [4096, 1024], P(('outer', 'inner')), may hold values from -6 to 6
- head_gain: float32 [1024], replicated, may hold values from 0.1 to 1.9
Outputs:
- attended: bfloat16 [4096, 1024], P(('outer', 'inner'))
The draws below stay inside these ranges and needn't reach their ends.
All inputs are finite; a program needn't handle non-finite values.
Results may differ from the reference program's by a relative error of at most 0.0034.
Values sent between devices are 32-bit elements; how exact they have to be, the bound alone decides.
No kernel may reach another device: no remote copies, remote signals or barrier semaphores. Data moves between devices by JAX's collectives and lax.ppermute only.
A program may use at most 64 MiB of HBM per device.

```python
import jax
import jax.numpy as jnp
from jax import lax

HEADS = 8
HEAD_DIM = 128
TOK_DEV = 128
WIDTH = 1024
TOKENS = 4096


def block_scale(own_key, dims, cuts, low, largest):
    loudness, own = 1.0, jax.random.fold_in(own_key, 6)
    for dim, shards_of in cuts:
        heights = jnp.exp(jax.random.uniform(jax.random.fold_in(own, dim), (shards_of,), jnp.float32, low / len(cuts), largest / len(cuts)))
        loudness = loudness * jnp.repeat(heights, dims[dim] // shards_of).reshape([-1 if axis == dim else 1 for axis in range(len(dims))])
    return loudness


def scatter_about(stream_key, extent, spread, most, pieces=(), held_as=jnp.bfloat16):
    drawn = jax.random.normal(stream_key, extent, jnp.float32) * spread
    if len(pieces) > 0:
        drawn = block_scale(stream_key, extent, pieces, -0.22, 0.18) * drawn
    return jnp.clip(drawn, min=-most, max=most).astype(held_as)


def setup_inputs(seed: int = 0) -> dict:
    seeds = jax.random.split(jax.random.key(seed), 5)
    return {
        "queries": scatter_about(seeds[0], (TOKENS, WIDTH), 1.0, 6.0, ((0, 32),)),
        "keys": scatter_about(seeds[1], (TOKENS, WIDTH), 1.0, 6.0, ((0, 32),)),
        "values": scatter_about(seeds[2], (TOKENS, WIDTH), 1.0, 6.0, ((0, 32),)),
        "head_gain": jnp.clip(1.0 + 0.18 * jax.random.normal(seeds[3], (WIDTH,), jnp.float32), 0.1, 1.9),
    }


def features(x):
    return (jax.nn.elu(x.astype(jnp.float32)) + 1.0).astype(jnp.bfloat16)

def reference(queries, keys, values, head_gain):
    blocks = TOKENS // TOK_DEV
    fq = features(queries).reshape(blocks, TOK_DEV, HEADS, HEAD_DIM)
    fk = features(keys).reshape(blocks, TOK_DEV, HEADS, HEAD_DIM)
    vals = values.reshape(blocks, TOK_DEV, HEADS, HEAD_DIM)
    causal = jnp.arange(TOK_DEV)[:, None] >= jnp.arange(TOK_DEV)[None, :]
    highest = lax.Precision.HIGHEST

    def step(carried, inputs):
        block_q, block_k, block_v = inputs
        query32 = block_q.astype(jnp.float32)
        key32 = block_k.astype(jnp.float32)
        value32 = block_v.astype(jnp.float32)
        own = jnp.einsum('thd,the->hde', key32, value32, precision=highest)
        rounded = lax.optimization_barrier(carried.astype(jnp.bfloat16)).astype(jnp.float32)
        inter = jnp.einsum('thd,hde->the', query32, rounded, precision=highest)
        scores = jnp.einsum('thd,shd->hts', query32, key32, precision=highest)
        weights = jnp.where(causal[None], scores, 0.0).astype(jnp.bfloat16)
        weights = lax.optimization_barrier(weights).astype(jnp.float32)
        intra = jnp.einsum('hts,she->the', weights, value32, precision=highest)
        total = inter + intra
        meansq = lax.optimization_barrier(jnp.mean(total * total, axis=-1, keepdims=True))
        normed = total * lax.rsqrt(meansq + 1e-06)
        result = (normed.reshape(TOK_DEV, WIDTH) * head_gain).astype(jnp.bfloat16)
        return (carried + own, result)
    start = jnp.zeros((HEADS, HEAD_DIM, HEAD_DIM), jnp.float32)
    _, outputs = lax.scan(step, start, (fq, fk, vals))
    return outputs.reshape(TOKENS, WIDTH)
```

```python
import functools

import jax
import jax.numpy as jnp
from jax import lax
from jax.experimental import pallas as pl
from jax.experimental.pallas import tpu as pltpu
from jax.sharding import PartitionSpec as P

HEADS = 8
HEAD_DIM = 128
HALF = HEADS // 2
CHUNKS = 2
AXES = ("outer", "inner")


def features(x):
    x = x.astype(jnp.float32)
    return jnp.where(x > 0.0, x + 1.0, jnp.exp(jnp.minimum(x, 0.0))).astype(jnp.bfloat16)


def head_cols(h):
    return pl.ds(pl.multiple_of(h * HEAD_DIM, HEAD_DIM), HEAD_DIM)


def state_kernel(core_ref, k_ref, v_ref, mine_ref, theirs_ref):
    core = core_ref[0]
    for half, out in ((1, theirs_ref), (0, mine_ref)):
        for i in range(HALF):
            h = (core * HALF + half * HALF + i) % HEADS
            fk = features(k_ref[:, head_cols(h)])
            out[i] = lax.dot_general(
                fk, v_ref[:, head_cols(h)], (((0,), (0,)), ((), ())), preferred_element_type=jnp.float32
            )


def intra_kernel(q_ref, k_ref, v_ref, fq_ref, intra_ref):
    rows = q_ref.shape[0]
    causal = lax.broadcasted_iota(jnp.int32, (rows, rows), 0) >= lax.broadcasted_iota(jnp.int32, (rows, rows), 1)
    for h in range(HEADS):
        cols = slice(h * HEAD_DIM, (h + 1) * HEAD_DIM)
        fq = features(q_ref[:, cols])
        fk = features(k_ref[:, cols])
        fq_ref[:, cols] = fq
        scores = lax.dot_general(fq, fk, (((1,), (1,)), ((), ())), preferred_element_type=jnp.float32)
        weights = jnp.where(causal, scores, 0.0).astype(jnp.bfloat16)
        intra_ref[:, cols] = jnp.dot(weights, v_ref[:, cols], preferred_element_type=jnp.float32)


def final_kernel(core_ref, fq_ref, intra_ref, gain_ref, *refs):
    carried, out_ref = refs[:-1], refs[-1]
    core = core_ref[0]
    per = HALF // CHUNKS
    for half in range(2):
        for c in range(CHUNKS):
            for i in range(per):
                h = (core * HALF + half * HALF + c * per + i) % HEADS
                state = carried[half * CHUNKS + c][i].astype(jnp.bfloat16)
                cols = head_cols(h)
                total = intra_ref[:, cols] + jnp.dot(fq_ref[:, cols], state, preferred_element_type=jnp.float32)
                meansq = jnp.mean(total * total, axis=-1, keepdims=True)
                out_ref[:, cols] = (total * lax.rsqrt(meansq + 1e-06) * gain_ref[:, cols]).astype(jnp.bfloat16)


VMEM = pl.BlockSpec(memory_space=pltpu.VMEM)
SMEM = pl.BlockSpec(memory_space=pltpu.SMEM)


def plan(outer, inner):
    assert outer % 2 == 0 and inner % 2 == 0
    y, x, z = (2, inner // 2), (inner, 2), (2 * inner, outer // 2)
    return y, x, z


def steps_of(level, kind):
    stride, radix = level
    if kind == "ring":
        return [("ring", level, s) for s in range(1, radix)]
    if radix <= 4:
        return [("chain", level, k) for k in range(radix - 1)]
    shifts = [1]
    reach = 1
    while reach < radix - 1:
        shifts.append(reach)
        reach *= 2
    return [("scan", level, s) for s in shifts]


def targets(step, i):
    kind, (stride, radix), s = step
    d = i // stride % radix
    if kind == "ring":
        return i + ((d + s) % radix - d) * stride
    if kind == "chain":
        return i + stride if d == s else None
    return i + s * stride if d + s < radix else None


def per_device(outer, inner, queries, keys, values, head_gain):
    rows = queries.shape[0]
    n = outer * inner
    me = lax.axis_index("outer") * inner + lax.axis_index("inner")
    core = me % 2
    upward = core == 0
    core_arr = core.reshape(1).astype(jnp.int32)
    f32 = jnp.float32
    mine, theirs = pl.pallas_call(
        state_kernel,
        out_shape=[jax.ShapeDtypeStruct((HALF, HEAD_DIM, HEAD_DIM), f32)] * 2,
        in_specs=[SMEM, VMEM, VMEM],
        out_specs=[VMEM, VMEM],
        name="own_state",
    )(core_arr, keys, values)
    fq, intra = pl.pallas_call(
        intra_kernel,
        out_shape=[
            jax.ShapeDtypeStruct(queries.shape, jnp.bfloat16),
            jax.ShapeDtypeStruct(queries.shape, f32),
        ],
        in_specs=[VMEM] * 3,
        out_specs=[VMEM] * 2,
        cost_estimate=pl.CostEstimate(
            flops=4 * HEADS * rows * rows * HEAD_DIM, bytes_accessed=6 * queries.size * 2, transcendentals=queries.size * 2
        ),
        name="intra",
    )(queries, keys, values)

    y, x, z = plan(outer, inner)
    up = steps_of(y, "ring") + steps_of(x, "ring") + steps_of(z, "line")
    down = steps_of(z, "line") + steps_of(x, "ring") + steps_of(y, "ring")
    swap = [(i, i ^ 1) for i in range(n)]
    perms = []
    for a, b in zip(up, down, strict=True):
        pairs = [(i, targets((a, b)[i % 2], i)) for i in range(n)]
        perms.append([(i, t) for i, t in pairs if t is not None])

    def digit(level):
        return me // level[0] % level[1]

    per = HALF // CHUNKS
    own_parts, other_parts = [], []
    for c in range(CHUNKS):
        part = slice(c * per, (c + 1) * per)
        mine_c = mine[part]
        partner = lax.ppermute(theirs[part], AXES, swap)
        base = mine_c + partner
        zero = jnp.zeros_like(base)
        before, total, carry = zero, base, zero
        level_total, level_carry = total, carry
        prev_a = prev_b = None
        for j, (a, b) in enumerate(zip(up, down, strict=True)):
            if prev_a != a[:2]:
                level_total, prev_a = total, a[:2]
            if prev_b != b[:2]:
                level_carry, prev_b = carry, b[:2]
            if a[0] == "ring":
                msg_a = level_total
            elif a[0] == "chain" or a[2] == 1 and (j == 0 or up[j - 1][0] != "scan"):
                msg_a = carry + total
            else:
                msg_a = carry
            if b[0] == "ring":
                msg_b = level_carry + jnp.where(digit(b[1]) + b[2] < b[1][1], base, zero)
            elif b[0] == "chain" or b[2] == 1 and (j == 0 or down[j - 1][0] != "scan"):
                msg_b = carry + base
            else:
                msg_b = carry
            got = lax.ppermute(jnp.where(upward, msg_a, msg_b), AXES, perms[j])
            if a[0] == "ring":
                before = before + jnp.where(upward & (digit(a[1]) >= a[2]), got, zero)
                total = total + got
                carry_a = carry
            else:
                carry_a = carry + got
            carry = jnp.where(upward, carry_a, carry + got)
        before_chip = before + carry
        own_parts.append(before_chip + jnp.where(upward, zero, partner))
        other_parts.append(lax.ppermute(before_chip + jnp.where(upward, mine_c, zero), AXES, swap))

    return pl.pallas_call(
        final_kernel,
        out_shape=jax.ShapeDtypeStruct(queries.shape, jnp.bfloat16),
        in_specs=[SMEM] + [VMEM] * (3 + 2 * CHUNKS),
        out_specs=VMEM,
        name="attend",
    )(core_arr, fq, intra, head_gain.reshape(1, -1), *own_parts, *other_parts)


def solution(mesh):
    outer, inner = mesh.shape["outer"], mesh.shape["inner"]
    return jax.shard_map(
        functools.partial(per_device, outer, inner),
        mesh=mesh,
        in_specs=(
            P(AXES, None),
            P(AXES, None),
            P(AXES, None),
            P(),
        ),
        out_specs=P(AXES, None),
        check_vma=False,
    )
```

```python
import functools

import jax
import jax.numpy as jnp
from jax import lax
from jax.experimental import pallas as pl
from jax.experimental.pallas import tpu as pltpu
from jax.sharding import PartitionSpec as P

HEADS = 8
HEAD_DIM = 128
HALF = HEADS // 2
CHUNKS = 2
PER = HALF // CHUNKS
AXES = ("outer", "inner")


def features(x):
    x = x.astype(jnp.float32)
    return jnp.where(x > 0.0, x + 1.0, jnp.exp(jnp.minimum(x, 0.0))).astype(jnp.bfloat16)


def head_cols(h):
    return pl.ds(pl.multiple_of(h * HEAD_DIM, HEAD_DIM), HEAD_DIM)


def state_kernel(core_ref, k_ref, v_ref, *out_refs):
    core = core_ref[0]
    for half in (1, 0):
        for i in range(HALF):
            h = (core * HALF + half * HALF + i) % HEADS
            fk = features(k_ref[:, head_cols(h)])
            out_refs[half * CHUNKS + i // PER][i % PER] = lax.dot_general(
                fk, v_ref[:, head_cols(h)], (((0,), (0,)), ((), ())), preferred_element_type=jnp.float32
            )


def intra_kernel(q_ref, k_ref, v_ref, fq_ref, intra_ref):
    rows = q_ref.shape[0]
    causal = lax.broadcasted_iota(jnp.int32, (rows, rows), 0) >= lax.broadcasted_iota(jnp.int32, (rows, rows), 1)
    for h in range(HEADS):
        cols = slice(h * HEAD_DIM, (h + 1) * HEAD_DIM)
        fq = features(q_ref[:, cols])
        fk = features(k_ref[:, cols])
        fq_ref[:, cols] = fq
        scores = lax.dot_general(fq, fk, (((1,), (1,)), ((), ())), preferred_element_type=jnp.float32)
        weights = jnp.where(causal, scores, 0.0).astype(jnp.bfloat16)
        intra_ref[:, cols] = jnp.dot(weights, v_ref[:, cols], preferred_element_type=jnp.float32)


def final_kernel(core_ref, fq_ref, intra_ref, gain_ref, *refs):
    carried, out_ref = refs[:-1], refs[-1]
    core = core_ref[0]
    for half in range(2):
        for c in range(CHUNKS):
            for i in range(PER):
                h = (core * HALF + half * HALF + c * PER + i) % HEADS
                state = carried[half * CHUNKS + c][i].astype(jnp.bfloat16)
                cols = head_cols(h)
                total = intra_ref[:, cols] + jnp.dot(fq_ref[:, cols], state, preferred_element_type=jnp.float32)
                meansq = jnp.mean(total * total, axis=-1, keepdims=True)
                out_ref[:, cols] = (total * lax.rsqrt(meansq + 1e-06) * gain_ref[:, cols]).astype(jnp.bfloat16)


VMEM = pl.BlockSpec(memory_space=pltpu.VMEM)
SMEM = pl.BlockSpec(memory_space=pltpu.SMEM)
PARAMS = pltpu.CompilerParams(vmem_limit_bytes=8 * 1024 * 1024)


def levels_of(stride, extent):
    levels = []
    while extent > 1:
        radix = next(r for r in range(2, extent + 1) if extent % r == 0)
        levels.append((stride, radix))
        stride, extent = stride * radix, extent // radix
    return levels


def steps_of(levels):
    return [(stride, radix, shift) for stride, radix in levels for shift in range(1, radix)]


def target(step, i):
    stride, radix, shift = step
    digit = i // stride % radix
    return i + ((digit + shift) % radix - digit) * stride


def per_device(outer, inner, queries, keys, values, head_gain):
    rows = queries.shape[0]
    n = outer * inner
    me = lax.axis_index("outer") * inner + lax.axis_index("inner")
    core = me % 2
    even = core == 0
    core_arr = core.reshape(1).astype(jnp.int32)
    f32 = jnp.float32
    part = jax.ShapeDtypeStruct((PER, HEAD_DIM, HEAD_DIM), f32)
    states = pl.pallas_call(
        state_kernel,
        out_shape=[part] * (2 * CHUNKS),
        in_specs=[SMEM, VMEM, VMEM],
        out_specs=[VMEM] * (2 * CHUNKS),
        compiler_params=PARAMS,
        name="own_state",
    )(core_arr, keys, values)
    fq, intra = pl.pallas_call(
        intra_kernel,
        out_shape=[
            jax.ShapeDtypeStruct(queries.shape, jnp.bfloat16),
            jax.ShapeDtypeStruct(queries.shape, f32),
        ],
        in_specs=[VMEM] * 3,
        out_specs=[VMEM] * 2,
        compiler_params=PARAMS,
        cost_estimate=pl.CostEstimate(
            flops=4 * HEADS * rows * rows * HEAD_DIM, bytes_accessed=6 * queries.size * 2, transcendentals=queries.size * 2
        ),
        name="intra",
    )(queries, keys, values)

    up_levels = levels_of(2, inner // 2) + levels_of(inner, outer)
    ups = steps_of(up_levels)
    downs = steps_of(up_levels[::-1])
    swap = [(i, i ^ 1) for i in range(n)]

    def digit(step):
        return me // step[0] % step[1]

    def to_swap(x):
        return lax.ppermute(x, AXES, swap)

    mine, theirs = states[:CHUNKS], states[CHUNKS:]
    partner = [to_swap(x) for x in theirs]
    own_parts, other_parts = [], []
    for c in range(CHUNKS):
        base = mine[c] + partner[c]
        zero = jnp.zeros_like(base)
        before, total = zero, base
        for j, (up, down) in enumerate(zip(ups, downs, strict=True)):
            if up[2] == 1:
                level_total = total
            if down[2] == 1:
                level_before = before
            higher = digit(down) + down[2] < down[1]
            message = jnp.where(even, level_total, level_before + jnp.where(higher, base, zero))
            perm = [(i, target(down if i % 2 else up, i)) for i in range(n)]
            got = lax.ppermute(message, AXES, perm)
            before = before + jnp.where(even & (digit(up) < up[2]), zero, got)
            total = total + got
        own_parts.append(before + jnp.where(even, zero, partner[c]))
        other_parts.append(to_swap(before + jnp.where(even, mine[c], zero)))

    return pl.pallas_call(
        final_kernel,
        out_shape=jax.ShapeDtypeStruct(queries.shape, jnp.bfloat16),
        in_specs=[SMEM] + [VMEM] * (3 + 2 * CHUNKS),
        out_specs=VMEM,
        compiler_params=PARAMS,
        name="attend",
    )(core_arr, fq, intra, head_gain.reshape(1, -1), *own_parts, *other_parts)


def solution(mesh):
    outer, inner = mesh.shape["outer"], mesh.shape["inner"]
    assert inner % 2 == 0
    return jax.shard_map(
        functools.partial(per_device, outer, inner),
        mesh=mesh,
        in_specs=(
            P(AXES, None),
            P(AXES, None),
            P(AXES, None),
            P(),
        ),
        out_specs=P(AXES, None),
        check_vma=False,
    )
```

```python
import functools

import jax
import jax.numpy as jnp
from jax import lax
from jax.experimental import pallas as pl
from jax.experimental.pallas import tpu as pltpu
from jax.sharding import PartitionSpec as P

HEADS = 8
HEAD_DIM = 128
HALF = HEADS // 2
CHUNKS = 2
PER = HALF // CHUNKS
AXES = ("outer", "inner")


def features(x):
    x = x.astype(jnp.float32)
    return jnp.where(x > 0.0, x + 1.0, jnp.exp(jnp.minimum(x, 0.0))).astype(jnp.bfloat16)


def head_cols(h):
    return pl.ds(pl.multiple_of(h * HEAD_DIM, HEAD_DIM), HEAD_DIM)


def state_kernel(core_ref, k_hbm, v_hbm, *refs):
    out_refs, (k_ref, v_ref, sems) = refs[: 2 * CHUNKS], refs[2 * CHUNKS :]
    copies = [
        pltpu.make_async_copy(k_hbm, k_ref, sems.at[0]),
        pltpu.make_async_copy(v_hbm, v_ref, sems.at[1]),
    ]
    for copy in copies:
        copy.start()
    for copy in copies:
        copy.wait()
    core = core_ref[0]
    for half in (1, 0):
        for i in range(HALF):
            h = (core * HALF + half * HALF + i) % HEADS
            fk = features(k_ref[:, head_cols(h)])
            out_refs[half * CHUNKS + i // PER][i % PER] = lax.dot_general(
                fk, v_ref[:, head_cols(h)], (((0,), (0,)), ((), ())), preferred_element_type=jnp.float32
            )


def intra_kernel(q_ref, k_ref, v_ref, late_ref, fq_ref, intra_ref):
    del late_ref
    rows = q_ref.shape[0]
    causal = lax.broadcasted_iota(jnp.int32, (rows, rows), 0) >= lax.broadcasted_iota(jnp.int32, (rows, rows), 1)
    for h in range(HEADS):
        cols = slice(h * HEAD_DIM, (h + 1) * HEAD_DIM)
        fq = features(q_ref[:, cols])
        fk = features(k_ref[:, cols])
        fq_ref[:, cols] = fq
        scores = lax.dot_general(fq, fk, (((1,), (1,)), ((), ())), preferred_element_type=jnp.float32)
        weights = jnp.where(causal, scores, 0.0).astype(jnp.bfloat16)
        intra_ref[:, cols] = jnp.dot(weights, v_ref[:, cols], preferred_element_type=jnp.float32)


def final_kernel(core_ref, fq_ref, intra_ref, gain_ref, *refs):
    carried, out_ref = refs[:-1], refs[-1]
    core = core_ref[0]
    for half in range(2):
        for c in range(CHUNKS):
            for i in range(PER):
                h = (core * HALF + half * HALF + c * PER + i) % HEADS
                state = carried[half * CHUNKS + c][i].astype(jnp.bfloat16)
                cols = head_cols(h)
                total = intra_ref[:, cols] + jnp.dot(fq_ref[:, cols], state, preferred_element_type=jnp.float32)
                meansq = jnp.mean(total * total, axis=-1, keepdims=True)
                out_ref[:, cols] = (total * lax.rsqrt(meansq + 1e-06) * gain_ref[:, cols]).astype(jnp.bfloat16)


VMEM = pl.BlockSpec(memory_space=pltpu.VMEM)
SMEM = pl.BlockSpec(memory_space=pltpu.SMEM)
HBM = pl.BlockSpec(memory_space=pltpu.HBM)
ANY = pl.BlockSpec(memory_space=pl.ANY)
PARAMS = pltpu.CompilerParams(vmem_limit_bytes=8 * 1024 * 1024)


def levels_of(stride, extent):
    levels = []
    while extent > 1:
        radix = next(r for r in range(2, extent + 1) if extent % r == 0)
        levels.append((stride, radix))
        stride, extent = stride * radix, extent // radix
    return levels


def steps_of(order):
    return [(kind, stride, radix, shift) for kind, (stride, radix) in order for shift in range(1, radix)]


def target(step, i):
    _, stride, radix, shift = step
    digit = i // stride % radix
    return i + ((digit + shift) % radix - digit) * stride


def per_device(outer, inner, queries, keys, values, head_gain):
    rows = queries.shape[0]
    n = outer * inner
    me = lax.axis_index("outer") * inner + lax.axis_index("inner")
    core = me % 2
    even = core == 0
    core_arr = core.reshape(1).astype(jnp.int32)
    f32 = jnp.float32
    part = jax.ShapeDtypeStruct((PER, HEAD_DIM, HEAD_DIM), f32)
    states = pl.pallas_call(
        state_kernel,
        out_shape=[part] * (2 * CHUNKS),
        in_specs=[SMEM, HBM, HBM],
        out_specs=[VMEM] * (2 * CHUNKS),
        scratch_shapes=[
            pltpu.VMEM(keys.shape, keys.dtype),
            pltpu.VMEM(values.shape, values.dtype),
            pltpu.SemaphoreType.DMA((2,)),
        ],
        compiler_params=PARAMS,
        name="own_state",
    )(core_arr, pltpu.with_memory_space_constraint(keys, pltpu.HBM), pltpu.with_memory_space_constraint(values, pltpu.HBM))
    low = levels_of(2, inner // 2)
    outer_levels = levels_of(inner, outer)
    low, high = low + outer_levels[:1], outer_levels[1:]
    total_low, total_high = [("total", v) for v in low], [("total", v) for v in high]
    prefix_low, prefix_high = [("prefix", v) for v in low[::-1]], [("prefix", v) for v in high[::-1]]
    orders = [
        (total_low + prefix_high, prefix_high + prefix_low),
        (total_low + total_high, total_high + prefix_low),
    ]
    swap = [(i, i ^ 1) for i in range(n)]

    def digit(step):
        return me // step[1] % step[2]

    def to_swap(x):
        return lax.ppermute(x, AXES, swap)

    mine, theirs = states[:CHUNKS], states[CHUNKS:]
    partner = [to_swap(x) for x in theirs]
    own_parts, other_parts = [], []
    late = None
    for c in range(CHUNKS):
        base = mine[c] + partner[c]
        zero = jnp.zeros_like(base)
        evens, odds = (steps_of(order) for order in orders[c % 2])
        before, apart, total, unit = zero, zero, base, base
        switched, entered = False, [None, None]
        for j, (up, down) in enumerate(zip(evens, odds, strict=True)):
            if up[0] == "prefix" and not switched:
                switched = True
                before, apart, unit = jnp.where(even, zero, before), jnp.where(even, before, zero), jnp.where(even, total, base)
            messages, kept = [], []
            for q, step in enumerate((up, down)):
                kind, _, radix, shift = step
                if shift == 1:
                    entered[q] = total if kind == "total" else before
                if kind == "total":
                    messages.append(entered[q])
                    kept.append(digit(step) >= shift)
                else:
                    messages.append(entered[q] + jnp.where(digit(step) + shift < radix, unit, zero))
                    kept.append(jnp.bool_(True))
            perm = [(i, target(down if i % 2 else up, i)) for i in range(n)]
            message = jnp.where(even, messages[0], messages[1])
            if c == CHUNKS - 1 and j == len(evens) - 1:
                late = message
            got = lax.ppermute(message, AXES, perm)
            before = before + jnp.where(jnp.where(even, kept[0], kept[1]), got, zero)
            total = total + got
        before = before + apart
        own_parts.append(before + jnp.where(even, zero, partner[c]))
        other_parts.append(to_swap(before + jnp.where(even, mine[c], zero)))

    fq, intra = pl.pallas_call(
        intra_kernel,
        out_shape=[
            jax.ShapeDtypeStruct(queries.shape, jnp.bfloat16),
            jax.ShapeDtypeStruct(queries.shape, f32),
        ],
        in_specs=[VMEM] * 3 + [ANY],
        out_specs=[VMEM] * 2,
        compiler_params=PARAMS,
        cost_estimate=pl.CostEstimate(
            flops=4 * HEADS * rows * rows * HEAD_DIM, bytes_accessed=6 * queries.size * 2, transcendentals=queries.size * 2
        ),
        name="intra",
    )(queries, keys, values, late)

    return pl.pallas_call(
        final_kernel,
        out_shape=jax.ShapeDtypeStruct(queries.shape, jnp.bfloat16),
        in_specs=[SMEM] + [VMEM] * (3 + 2 * CHUNKS),
        out_specs=VMEM,
        compiler_params=PARAMS,
        name="attend",
    )(core_arr, fq, intra, head_gain.reshape(1, -1), *own_parts, *other_parts)


def solution(mesh):
    outer, inner = mesh.shape["outer"], mesh.shape["inner"]
    assert inner % 2 == 0
    return jax.shard_map(
        functools.partial(per_device, outer, inner),
        mesh=mesh,
        in_specs=(
            P(AXES, None),
            P(AXES, None),
            P(AXES, None),
            P(),
        ),
        out_specs=P(AXES, None),
        check_vma=False,
    )
```

```python
import functools

import jax
import jax.numpy as jnp
from jax import lax
from jax.experimental import pallas as pl
from jax.experimental.pallas import tpu as pltpu
from jax.sharding import PartitionSpec as P

HEADS = 8
HEAD_DIM = 128
HALF = HEADS // 2
CHUNKS = 2
PER = HALF // CHUNKS
AXES = ("outer", "inner")


def features(x):
    x = x.astype(jnp.float32)
    return jnp.where(x > 0.0, x + 1.0, jnp.exp(jnp.minimum(x, 0.0))).astype(jnp.bfloat16)


def head_cols(h):
    return pl.ds(pl.multiple_of(h * HEAD_DIM, HEAD_DIM), HEAD_DIM)


def state_kernel(core_ref, k_hbm, v_hbm, *refs):
    out_refs, (k_ref, v_ref, sems) = refs[: 2 * CHUNKS], refs[2 * CHUNKS :]
    copies = [
        pltpu.make_async_copy(k_hbm, k_ref, sems.at[0]),
        pltpu.make_async_copy(v_hbm, v_ref, sems.at[1]),
    ]
    for copy in copies:
        copy.start()
    for copy in copies:
        copy.wait()
    core = core_ref[0]
    for half in (1, 0):
        for i in range(HALF):
            h = (core * HALF + half * HALF + i) % HEADS
            fk = features(k_ref[:, head_cols(h)])
            out_refs[half * CHUNKS + i // PER][i % PER] = lax.dot_general(
                fk, v_ref[:, head_cols(h)], (((0,), (0,)), ((), ())), preferred_element_type=jnp.float32
            )


def intra_kernel(q_ref, k_ref, v_ref, late_ref, fq_ref, intra_ref):
    del late_ref
    rows = q_ref.shape[0]
    causal = lax.broadcasted_iota(jnp.int32, (rows, rows), 0) >= lax.broadcasted_iota(jnp.int32, (rows, rows), 1)
    for h in range(HEADS):
        cols = slice(h * HEAD_DIM, (h + 1) * HEAD_DIM)
        fq = features(q_ref[:, cols])
        fk = features(k_ref[:, cols])
        fq_ref[:, cols] = fq
        scores = lax.dot_general(fq, fk, (((1,), (1,)), ((), ())), preferred_element_type=jnp.float32)
        weights = jnp.where(causal, scores, 0.0).astype(jnp.bfloat16)
        intra_ref[:, cols] = jnp.dot(weights, v_ref[:, cols], preferred_element_type=jnp.float32)


def attend_kernel(jobs, core_ref, fq_ref, intra_ref, gain_ref, *refs):
    carried, (out_hbm, buf_ref, sems) = refs[: len(jobs)], refs[-3:]
    core = core_ref[0]
    copies = []
    for slot, (half, c) in enumerate(jobs):
        first = (core * HALF + half * HALF + c * PER) % HEADS
        for i in range(PER):
            cols = head_cols(first + i)
            state = carried[slot][i].astype(jnp.bfloat16)
            total = intra_ref[:, cols] + jnp.dot(fq_ref[:, cols], state, preferred_element_type=jnp.float32)
            meansq = jnp.mean(total * total, axis=-1, keepdims=True)
            normed = total * lax.rsqrt(meansq + 1e-06) * gain_ref[:, cols]
            buf_ref[slot, :, i * HEAD_DIM : (i + 1) * HEAD_DIM] = normed.astype(jnp.bfloat16)
        width = PER * HEAD_DIM
        place = pl.ds(pl.multiple_of(first * HEAD_DIM, width), width)
        copy = pltpu.make_async_copy(buf_ref.at[slot], out_hbm.at[:, place], sems.at[slot])
        copy.start()
        copies.append(copy)
    for copy in copies:
        copy.wait()


VMEM = pl.BlockSpec(memory_space=pltpu.VMEM)
SMEM = pl.BlockSpec(memory_space=pltpu.SMEM)
HBM = pl.BlockSpec(memory_space=pltpu.HBM)
ANY = pl.BlockSpec(memory_space=pl.ANY)
PARAMS = pltpu.CompilerParams(vmem_limit_bytes=8 * 1024 * 1024)


def levels_of(stride, extent):
    levels = []
    while extent > 1:
        radix = next(r for r in range(2, extent + 1) if extent % r == 0)
        levels.append((stride, radix))
        stride, extent = stride * radix, extent // radix
    return levels


def steps_of(order):
    return [(kind, stride, radix, shift) for kind, (stride, radix) in order for shift in range(1, radix)]


def target(step, i):
    _, stride, radix, shift = step
    digit = i // stride % radix
    return i + ((digit + shift) % radix - digit) * stride


def per_device(outer, inner, queries, keys, values, head_gain):
    rows = queries.shape[0]
    n = outer * inner
    me = lax.axis_index("outer") * inner + lax.axis_index("inner")
    core = me % 2
    even = core == 0
    core_arr = core.reshape(1).astype(jnp.int32)
    f32 = jnp.float32
    part = jax.ShapeDtypeStruct((PER, HEAD_DIM, HEAD_DIM), f32)
    states = pl.pallas_call(
        state_kernel,
        out_shape=[part] * (2 * CHUNKS),
        in_specs=[SMEM, HBM, HBM],
        out_specs=[VMEM] * (2 * CHUNKS),
        scratch_shapes=[
            pltpu.VMEM(keys.shape, keys.dtype),
            pltpu.VMEM(values.shape, values.dtype),
            pltpu.SemaphoreType.DMA((2,)),
        ],
        compiler_params=PARAMS,
        name="own_state",
    )(core_arr, pltpu.with_memory_space_constraint(keys, pltpu.HBM), pltpu.with_memory_space_constraint(values, pltpu.HBM))
    low = levels_of(2, inner // 2)
    outer_levels = levels_of(inner, outer)
    low, high = low + outer_levels[:1], outer_levels[1:]
    total_low, total_high = [("total", v) for v in low], [("total", v) for v in high]
    prefix_low, prefix_high = [("prefix", v) for v in low[::-1]], [("prefix", v) for v in high[::-1]]
    orders = [
        (total_low + prefix_high, prefix_high + prefix_low),
        (total_low + total_high, total_high + prefix_low),
    ]
    swap = [(i, i ^ 1) for i in range(n)]

    def digit(step):
        return me // step[1] % step[2]

    def to_swap(x):
        return lax.ppermute(x, AXES, swap)

    mine, theirs = states[:CHUNKS], states[CHUNKS:]
    partner = [to_swap(x) for x in theirs]
    own_parts, other_parts = [], []
    late = None
    for c in range(CHUNKS):
        base = mine[c] + partner[c]
        zero = jnp.zeros_like(base)
        evens, odds = (steps_of(order) for order in orders[c % 2])
        before, apart, total, unit = zero, zero, base, base
        switched, entered = False, [None, None]
        for j, (up, down) in enumerate(zip(evens, odds, strict=True)):
            if up[0] == "prefix" and not switched:
                switched = True
                before, apart, unit = jnp.where(even, zero, before), jnp.where(even, before, zero), jnp.where(even, total, base)
            messages, kept = [], []
            for q, step in enumerate((up, down)):
                kind, _, radix, shift = step
                if shift == 1:
                    entered[q] = total if kind == "total" else before
                if kind == "total":
                    messages.append(entered[q])
                    kept.append(digit(step) >= shift)
                else:
                    messages.append(entered[q] + jnp.where(digit(step) + shift < radix, unit, zero))
                    kept.append(jnp.bool_(True))
            perm = [(i, target(down if i % 2 else up, i)) for i in range(n)]
            message = jnp.where(even, messages[0], messages[1])
            if c == CHUNKS - 1 and j == len(evens) - 1:
                late = message
            got = lax.ppermute(message, AXES, perm)
            before = before + jnp.where(jnp.where(even, kept[0], kept[1]), got, zero)
            total = total + got
        before = before + apart
        own_parts.append(before + jnp.where(even, zero, partner[c]))
        other_parts.append(to_swap(before + jnp.where(even, mine[c], zero)))

    fq, intra = pl.pallas_call(
        intra_kernel,
        out_shape=[
            jax.ShapeDtypeStruct(queries.shape, jnp.bfloat16),
            jax.ShapeDtypeStruct(queries.shape, f32),
        ],
        in_specs=[VMEM] * 3 + [ANY],
        out_specs=[VMEM] * 2,
        compiler_params=PARAMS,
        cost_estimate=pl.CostEstimate(
            flops=4 * HEADS * rows * rows * HEAD_DIM, bytes_accessed=6 * queries.size * 2, transcendentals=queries.size * 2
        ),
        name="intra",
    )(queries, keys, values, late)

    gain = head_gain.reshape(1, -1)

    def attend(jobs, parts, so_far=None):
        whole = jax.ShapeDtypeStruct(queries.shape, jnp.bfloat16)
        extra = [] if so_far is None else [so_far]
        given = [core_arr, fq, intra, gain, *parts, *extra]
        return pl.pallas_call(
            functools.partial(attend_kernel, jobs),
            out_shape=whole,
            in_specs=[SMEM] + [VMEM] * (3 + len(jobs)) + [HBM] * len(extra),
            out_specs=HBM,
            scratch_shapes=[
                pltpu.VMEM((len(jobs), rows, PER * HEAD_DIM), jnp.bfloat16),
                pltpu.SemaphoreType.DMA((len(jobs),)),
            ],
            input_output_aliases={len(given) - 1: 0} if extra else {},
            compiler_params=PARAMS,
            cost_estimate=pl.CostEstimate(
                flops=2 * len(jobs) * PER * rows * HEAD_DIM * HEAD_DIM, bytes_accessed=len(jobs) * queries.size, transcendentals=0
            ),
            name="attend",
        )(*given)

    early = [(0, c) for c in range(CHUNKS)] + [(1, c) for c in range(1, CHUNKS)]
    most = attend(early, own_parts + other_parts[1:])
    return attend([(1, 0)], other_parts[:1], most)


def solution(mesh):
    outer, inner = mesh.shape["outer"], mesh.shape["inner"]
    assert inner % 2 == 0
    return jax.shard_map(
        functools.partial(per_device, outer, inner),
        mesh=mesh,
        in_specs=(
            P(AXES, None),
            P(AXES, None),
            P(AXES, None),
            P(),
        ),
        out_specs=P(AXES, None),
        check_vma=False,
    )
```

```python
import functools

import jax
import jax.numpy as jnp
from jax import lax
from jax.experimental import pallas as pl
from jax.experimental.pallas import tpu as pltpu
from jax.sharding import PartitionSpec as P

HEADS = 8
HEAD_DIM = 128
HALF = HEADS // 2
CHUNKS = 2
PER = HALF // CHUNKS
AXES = ("outer", "inner")


def features(x):
    x = x.astype(jnp.float32)
    return jnp.where(x > 0.0, x + 1.0, jnp.exp(jnp.minimum(x, 0.0))).astype(jnp.bfloat16)


def head_cols(h):
    return pl.ds(pl.multiple_of(h * HEAD_DIM, HEAD_DIM), HEAD_DIM)


def state_kernel(core_ref, k_hbm, v_hbm, *refs):
    out_refs, (k_ref, v_ref, sems) = refs[: 2 * CHUNKS], refs[2 * CHUNKS :]
    core = core_ref[0]
    width = HALF * HEAD_DIM
    copies = {}
    for half in (1, 0):
        cols = pl.ds(pl.multiple_of((core + half) % 2 * width, width), width)
        copies[half] = [
            pltpu.make_async_copy(k_hbm.at[:, cols], k_ref.at[half], sems.at[half, 0]),
            pltpu.make_async_copy(v_hbm.at[:, cols], v_ref.at[half], sems.at[half, 1]),
        ]
        for copy in copies[half]:
            copy.start()
    for half in (1, 0):
        for copy in copies[half]:
            copy.wait()
        for i in range(HALF):
            cols = slice(i * HEAD_DIM, (i + 1) * HEAD_DIM)
            fk = features(k_ref[half, :, cols])
            out_refs[half * CHUNKS + i // PER][i % PER] = lax.dot_general(
                fk, v_ref[half, :, cols], (((0,), (0,)), ((), ())), preferred_element_type=jnp.float32
            )


def intra_kernel(q_ref, k_ref, v_ref, gain_ref, late_ref, fq_ref, intra_ref, near_gain_ref):
    del late_ref
    near_gain_ref[...] = gain_ref[...]
    rows = q_ref.shape[0]
    causal = lax.broadcasted_iota(jnp.int32, (rows, rows), 0) >= lax.broadcasted_iota(jnp.int32, (rows, rows), 1)
    for h in range(HEADS):
        cols = slice(h * HEAD_DIM, (h + 1) * HEAD_DIM)
        fq = features(q_ref[:, cols])
        fk = features(k_ref[:, cols])
        fq_ref[:, cols] = fq
        scores = lax.dot_general(fq, fk, (((1,), (1,)), ((), ())), preferred_element_type=jnp.float32)
        weights = jnp.where(causal, scores, 0.0).astype(jnp.bfloat16)
        intra_ref[:, cols] = jnp.dot(weights, v_ref[:, cols], preferred_element_type=jnp.float32)


def attend_kernel(jobs, core_ref, fq_ref, intra_ref, gain_ref, *refs):
    carried, (out_hbm, buf_ref, sems) = refs[: len(jobs)], refs[-3:]
    core = core_ref[0]
    copies = []
    for slot, (half, c) in enumerate(jobs):
        first = (core * HALF + half * HALF + c * PER) % HEADS
        for i in range(PER):
            cols = head_cols(first + i)
            state = carried[slot][i].astype(jnp.bfloat16)
            total = intra_ref[:, cols] + jnp.dot(fq_ref[:, cols], state, preferred_element_type=jnp.float32)
            meansq = jnp.mean(total * total, axis=-1, keepdims=True)
            normed = total * lax.rsqrt(meansq + 1e-06) * gain_ref[:, cols]
            buf_ref[slot, :, i * HEAD_DIM : (i + 1) * HEAD_DIM] = normed.astype(jnp.bfloat16)
        width = PER * HEAD_DIM
        place = pl.ds(pl.multiple_of(first * HEAD_DIM, width), width)
        copy = pltpu.make_async_copy(buf_ref.at[slot], out_hbm.at[:, place], sems.at[slot])
        copy.start()
        copies.append(copy)
    for copy in copies:
        copy.wait()


VMEM = pl.BlockSpec(memory_space=pltpu.VMEM)
SMEM = pl.BlockSpec(memory_space=pltpu.SMEM)
HBM = pl.BlockSpec(memory_space=pltpu.HBM)
ANY = pl.BlockSpec(memory_space=pl.ANY)
PARAMS = pltpu.CompilerParams(vmem_limit_bytes=8 * 1024 * 1024)


def levels_of(stride, extent):
    levels = []
    while extent > 1:
        radix = next(r for r in range(2, extent + 1) if extent % r == 0)
        levels.append((stride, radix))
        stride, extent = stride * radix, extent // radix
    return levels


def steps_of(order):
    return [(kind, stride, radix, shift) for kind, (stride, radix) in order for shift in range(1, radix)]


def target(step, i):
    _, stride, radix, shift = step
    digit = i // stride % radix
    return i + ((digit + shift) % radix - digit) * stride


def per_device(outer, inner, queries, keys, values, head_gain):
    rows = queries.shape[0]
    n = outer * inner
    me = lax.axis_index("outer") * inner + lax.axis_index("inner")
    core = me % 2
    even = core == 0
    core_arr = core.reshape(1).astype(jnp.int32)
    f32 = jnp.float32
    part = jax.ShapeDtypeStruct((PER, HEAD_DIM, HEAD_DIM), f32)
    states = pl.pallas_call(
        state_kernel,
        out_shape=[part] * (2 * CHUNKS),
        in_specs=[SMEM, HBM, HBM],
        out_specs=[VMEM] * (2 * CHUNKS),
        scratch_shapes=[
            pltpu.VMEM((2, rows, HALF * HEAD_DIM), keys.dtype),
            pltpu.VMEM((2, rows, HALF * HEAD_DIM), values.dtype),
            pltpu.SemaphoreType.DMA((2, 2)),
        ],
        compiler_params=PARAMS,
        name="own_state",
    )(core_arr, pltpu.with_memory_space_constraint(keys, pltpu.HBM), pltpu.with_memory_space_constraint(values, pltpu.HBM))
    low = levels_of(2, inner // 2)
    outer_levels = levels_of(inner, outer)
    low, high = low + outer_levels[:1], outer_levels[1:]
    total_low, total_high = [("total", v) for v in low], [("total", v) for v in high]
    prefix_low, prefix_high = [("prefix", v) for v in low[::-1]], [("prefix", v) for v in high[::-1]]
    orders = [
        (total_low + prefix_high, prefix_high + prefix_low),
        (total_low + total_high, total_high + prefix_low),
    ]
    swap = [(i, i ^ 1) for i in range(n)]

    def digit(step):
        return me // step[1] % step[2]

    def to_swap(x):
        return lax.ppermute(x, AXES, swap)

    mine, theirs = states[:CHUNKS], states[CHUNKS:]
    partner = [to_swap(x) for x in theirs]
    own_parts, other_parts = [], []
    late = None
    for c in range(CHUNKS):
        base = mine[c] + partner[c]
        zero = jnp.zeros_like(base)
        evens, odds = (steps_of(order) for order in orders[c % 2])
        before, apart, total, unit = zero, zero, base, base
        switched, entered = False, [None, None]
        for j, (up, down) in enumerate(zip(evens, odds, strict=True)):
            if up[0] == "prefix" and not switched:
                switched = True
                before, apart, unit = jnp.where(even, zero, before), jnp.where(even, before, zero), jnp.where(even, total, base)
            messages, kept = [], []
            for q, step in enumerate((up, down)):
                kind, _, radix, shift = step
                if shift == 1:
                    entered[q] = total if kind == "total" else before
                if kind == "total":
                    messages.append(entered[q])
                    kept.append(digit(step) >= shift)
                else:
                    messages.append(entered[q] + jnp.where(digit(step) + shift < radix, unit, zero))
                    kept.append(jnp.bool_(True))
            perm = [(i, target(down if i % 2 else up, i)) for i in range(n)]
            message = jnp.where(even, messages[0], messages[1])
            if c == CHUNKS - 1 and j == len(evens) - 1:
                late = message
            got = lax.ppermute(message, AXES, perm)
            before = before + jnp.where(jnp.where(even, kept[0], kept[1]), got, zero)
            total = total + got
        before = before + apart
        own_parts.append(before + jnp.where(even, zero, partner[c]))
        other_parts.append(to_swap(before + jnp.where(even, mine[c], zero)))

    fq, intra, gain = pl.pallas_call(
        intra_kernel,
        out_shape=[
            jax.ShapeDtypeStruct(queries.shape, jnp.bfloat16),
            jax.ShapeDtypeStruct(queries.shape, f32),
            jax.ShapeDtypeStruct((1, queries.shape[1]), f32),
        ],
        in_specs=[VMEM] * 4 + [ANY],
        out_specs=[VMEM] * 3,
        compiler_params=PARAMS,
        cost_estimate=pl.CostEstimate(
            flops=4 * HEADS * rows * rows * HEAD_DIM, bytes_accessed=6 * queries.size * 2, transcendentals=queries.size * 2
        ),
        name="intra",
    )(queries, keys, values, head_gain.reshape(1, -1), late)

    def attend(jobs, parts, so_far=None):
        whole = jax.ShapeDtypeStruct(queries.shape, jnp.bfloat16)
        extra = [] if so_far is None else [so_far]
        given = [core_arr, fq, intra, gain, *parts, *extra]
        return pl.pallas_call(
            functools.partial(attend_kernel, jobs),
            out_shape=whole,
            in_specs=[SMEM] + [VMEM] * (3 + len(jobs)) + [HBM] * len(extra),
            out_specs=HBM,
            scratch_shapes=[
                pltpu.VMEM((len(jobs), rows, PER * HEAD_DIM), jnp.bfloat16),
                pltpu.SemaphoreType.DMA((len(jobs),)),
            ],
            input_output_aliases={len(given) - 1: 0} if extra else {},
            compiler_params=PARAMS,
            cost_estimate=pl.CostEstimate(
                flops=2 * len(jobs) * PER * rows * HEAD_DIM * HEAD_DIM, bytes_accessed=len(jobs) * queries.size, transcendentals=0
            ),
            name="attend",
        )(*given)

    early = [(0, c) for c in range(CHUNKS)] + [(1, c) for c in range(1, CHUNKS)]
    most = attend(early, own_parts + other_parts[1:])
    return attend([(1, 0)], other_parts[:1], most)


def solution(mesh):
    outer, inner = mesh.shape["outer"], mesh.shape["inner"]
    assert inner % 2 == 0
    return jax.shard_map(
        functools.partial(per_device, outer, inner),
        mesh=mesh,
        in_specs=(
            P(AXES, None),
            P(AXES, None),
            P(AXES, None),
            P(),
        ),
        out_specs=P(AXES, None),
        check_vma=False,
    )
```

```python
import functools

import jax
import jax.numpy as jnp
from jax import lax
from jax.experimental import pallas as pl
from jax.experimental.pallas import tpu as pltpu
from jax.sharding import PartitionSpec as P

HEADS = 8
HEAD_DIM = 128
HALF = HEADS // 2
CHUNKS = 2
PER = HALF // CHUNKS
AXES = ("outer", "inner")


def features(x):
    x = x.astype(jnp.float32)
    return jnp.where(x > 0.0, x + 1.0, jnp.exp(jnp.minimum(x, 0.0))).astype(jnp.bfloat16)


def head_cols(h):
    return pl.ds(pl.multiple_of(h * HEAD_DIM, HEAD_DIM), HEAD_DIM)


def states_of(half, core, k_ref, v_ref, out_refs):
    for i in range(HALF):
        cols = head_cols((core * HALF + half * HALF + i) % HEADS)
        fk = features(k_ref[:, cols])
        out_refs[i // PER][i % PER] = lax.dot_general(
            fk, v_ref[:, cols], (((0,), (0,)), ((), ())), preferred_element_type=jnp.float32
        )


def theirs_kernel(core_ref, k_hbm, v_hbm, *refs):
    out_refs, (k_ref, v_ref, sems) = refs[:CHUNKS], refs[CHUNKS:]
    copies = [
        pltpu.make_async_copy(k_hbm, k_ref, sems.at[0]),
        pltpu.make_async_copy(v_hbm, v_ref, sems.at[1]),
    ]
    for copy in copies:
        copy.start()
    for copy in copies:
        copy.wait()
    states_of(1, core_ref[0], k_ref, v_ref, out_refs)


def mine_kernel(core_ref, k_ref, v_ref, *out_refs):
    states_of(0, core_ref[0], k_ref, v_ref, out_refs)


def intra_kernel(q_ref, k_ref, v_ref, gain_ref, late_ref, fq_ref, intra_ref, near_gain_ref):
    del late_ref
    near_gain_ref[...] = gain_ref[...]
    rows = q_ref.shape[0]
    causal = lax.broadcasted_iota(jnp.int32, (rows, rows), 0) >= lax.broadcasted_iota(jnp.int32, (rows, rows), 1)
    for h in range(HEADS):
        cols = slice(h * HEAD_DIM, (h + 1) * HEAD_DIM)
        fq = features(q_ref[:, cols])
        fk = features(k_ref[:, cols])
        fq_ref[:, cols] = fq
        scores = lax.dot_general(fq, fk, (((1,), (1,)), ((), ())), preferred_element_type=jnp.float32)
        weights = jnp.where(causal, scores, 0.0).astype(jnp.bfloat16)
        intra_ref[:, cols] = jnp.dot(weights, v_ref[:, cols], preferred_element_type=jnp.float32)


def attend_kernel(jobs, core_ref, fq_ref, intra_ref, gain_ref, *refs):
    carried, (out_hbm, buf_ref, sems) = refs[: len(jobs)], refs[-3:]
    core = core_ref[0]
    copies = []
    for slot, (half, c) in enumerate(jobs):
        first = (core * HALF + half * HALF + c * PER) % HEADS
        for i in range(PER):
            cols = head_cols(first + i)
            state = carried[slot][i].astype(jnp.bfloat16)
            total = intra_ref[:, cols] + jnp.dot(fq_ref[:, cols], state, preferred_element_type=jnp.float32)
            meansq = jnp.mean(total * total, axis=-1, keepdims=True)
            normed = total * lax.rsqrt(meansq + 1e-06) * gain_ref[:, cols]
            buf_ref[slot, :, i * HEAD_DIM : (i + 1) * HEAD_DIM] = normed.astype(jnp.bfloat16)
        width = PER * HEAD_DIM
        place = pl.ds(pl.multiple_of(first * HEAD_DIM, width), width)
        copy = pltpu.make_async_copy(buf_ref.at[slot], out_hbm.at[:, place], sems.at[slot])
        copy.start()
        copies.append(copy)
    for copy in copies:
        copy.wait()


VMEM = pl.BlockSpec(memory_space=pltpu.VMEM)
SMEM = pl.BlockSpec(memory_space=pltpu.SMEM)
HBM = pl.BlockSpec(memory_space=pltpu.HBM)
ANY = pl.BlockSpec(memory_space=pl.ANY)
PARAMS = pltpu.CompilerParams(vmem_limit_bytes=8 * 1024 * 1024)


def levels_of(stride, extent):
    levels = []
    while extent > 1:
        radix = next(r for r in range(2, extent + 1) if extent % r == 0)
        levels.append((stride, radix))
        stride, extent = stride * radix, extent // radix
    return levels


def steps_of(order):
    return [(kind, stride, radix, shift) for kind, (stride, radix) in order for shift in range(1, radix)]


def target(step, i):
    _, stride, radix, shift = step
    digit = i // stride % radix
    return i + ((digit + shift) % radix - digit) * stride


def per_device(outer, inner, queries, keys, values, head_gain):
    rows = queries.shape[0]
    n = outer * inner
    me = lax.axis_index("outer") * inner + lax.axis_index("inner")
    core = me % 2
    even = core == 0
    core_arr = core.reshape(1).astype(jnp.int32)
    f32 = jnp.float32
    part = jax.ShapeDtypeStruct((PER, HEAD_DIM, HEAD_DIM), f32)
    *theirs, near_keys, near_values = pl.pallas_call(
        theirs_kernel,
        out_shape=[part] * CHUNKS + [jax.ShapeDtypeStruct(x.shape, x.dtype) for x in (keys, values)],
        in_specs=[SMEM, HBM, HBM],
        out_specs=[VMEM] * (CHUNKS + 2),
        scratch_shapes=[pltpu.SemaphoreType.DMA((2,))],
        compiler_params=PARAMS,
        name="theirs",
    )(
        core_arr,
        pltpu.with_memory_space_constraint(keys, pltpu.HBM),
        pltpu.with_memory_space_constraint(values, pltpu.HBM),
    )
    mine = pl.pallas_call(
        mine_kernel,
        out_shape=[part] * CHUNKS,
        in_specs=[SMEM, VMEM, VMEM],
        out_specs=[VMEM] * CHUNKS,
        compiler_params=PARAMS,
        cost_estimate=pl.CostEstimate(
            flops=2 * HALF * rows * HEAD_DIM * HEAD_DIM, bytes_accessed=4 * keys.size, transcendentals=keys.size // 2
        ),
        name="mine",
    )(core_arr, near_keys, near_values)

    low = levels_of(2, inner // 2)
    outer_levels = levels_of(inner, outer)
    low, high = low + outer_levels[:1], outer_levels[1:]
    total_low, total_high = [("total", v) for v in low], [("total", v) for v in high]
    prefix_low, prefix_high = [("prefix", v) for v in low[::-1]], [("prefix", v) for v in high[::-1]]
    orders = [
        (total_low + prefix_high, prefix_high + prefix_low),
        (total_low + total_high, total_high + prefix_low),
    ]
    swap = [(i, i ^ 1) for i in range(n)]

    def digit(step):
        return me // step[1] % step[2]

    def to_swap(x):
        return lax.ppermute(x, AXES, swap)

    partner = [to_swap(x) for x in theirs]
    own_parts, other_parts = [], []
    late = None
    for c in range(CHUNKS):
        base = mine[c] + partner[c]
        zero = jnp.zeros_like(base)
        evens, odds = (steps_of(order) for order in orders[c % 2])
        before, apart, total, unit = zero, zero, base, base
        switched, entered = False, [None, None]
        for j, (up, down) in enumerate(zip(evens, odds, strict=True)):
            if up[0] == "prefix" and not switched:
                switched = True
                before, apart, unit = jnp.where(even, zero, before), jnp.where(even, before, zero), jnp.where(even, total, base)
            messages, kept = [], []
            for q, step in enumerate((up, down)):
                kind, _, radix, shift = step
                if shift == 1:
                    entered[q] = total if kind == "total" else before
                if kind == "total":
                    messages.append(entered[q])
                    kept.append(digit(step) >= shift)
                else:
                    messages.append(entered[q] + jnp.where(digit(step) + shift < radix, unit, zero))
                    kept.append(jnp.bool_(True))
            perm = [(i, target(down if i % 2 else up, i)) for i in range(n)]
            message = jnp.where(even, messages[0], messages[1])
            if c == CHUNKS - 1 and j == len(evens) - 1:
                late = message
            got = lax.ppermute(message, AXES, perm)
            before = before + jnp.where(jnp.where(even, kept[0], kept[1]), got, zero)
            total = total + got
        before = before + apart
        own_parts.append(before + jnp.where(even, zero, partner[c]))
        other_parts.append(to_swap(before + jnp.where(even, mine[c], zero)))

    fq, intra, gain = pl.pallas_call(
        intra_kernel,
        out_shape=[
            jax.ShapeDtypeStruct(queries.shape, jnp.bfloat16),
            jax.ShapeDtypeStruct(queries.shape, f32),
            jax.ShapeDtypeStruct((1, queries.shape[1]), f32),
        ],
        in_specs=[VMEM] * 4 + [ANY],
        out_specs=[VMEM] * 3,
        compiler_params=PARAMS,
        cost_estimate=pl.CostEstimate(
            flops=4 * HEADS * rows * rows * HEAD_DIM, bytes_accessed=6 * queries.size * 2, transcendentals=queries.size * 2
        ),
        name="intra",
    )(queries, near_keys, near_values, head_gain.reshape(1, -1), late)

    def attend(jobs, parts, so_far=None):
        whole = jax.ShapeDtypeStruct(queries.shape, jnp.bfloat16)
        extra = [] if so_far is None else [so_far]
        given = [core_arr, fq, intra, gain, *parts, *extra]
        return pl.pallas_call(
            functools.partial(attend_kernel, jobs),
            out_shape=whole,
            in_specs=[SMEM] + [VMEM] * (3 + len(jobs)) + [HBM] * len(extra),
            out_specs=HBM,
            scratch_shapes=[
                pltpu.VMEM((len(jobs), rows, PER * HEAD_DIM), jnp.bfloat16),
                pltpu.SemaphoreType.DMA((len(jobs),)),
            ],
            input_output_aliases={len(given) - 1: 0} if extra else {},
            compiler_params=PARAMS,
            cost_estimate=pl.CostEstimate(
                flops=2 * len(jobs) * PER * rows * HEAD_DIM * HEAD_DIM, bytes_accessed=len(jobs) * queries.size, transcendentals=0
            ),
            name="attend",
        )(*given)

    early = [(0, c) for c in range(CHUNKS)] + [(1, c) for c in range(1, CHUNKS)]
    most = attend(early, own_parts + other_parts[1:])
    return attend([(1, 0)], other_parts[:1], most)


def solution(mesh):
    outer, inner = mesh.shape["outer"], mesh.shape["inner"]
    assert inner % 2 == 0
    return jax.shard_map(
        functools.partial(per_device, outer, inner),
        mesh=mesh,
        in_specs=(
            P(AXES, None),
            P(AXES, None),
            P(AXES, None),
            P(),
        ),
        out_specs=P(AXES, None),
        check_vma=False,
    )
```

```python
import functools
import itertools

import jax
import jax.numpy as jnp
from jax import lax
from jax.experimental import pallas as pl
from jax.experimental.pallas import tpu as pltpu
from jax.sharding import PartitionSpec as P

HEADS = 8
HEAD_DIM = 128
HALF = HEADS // 2
CHUNKS = 2
PER = HALF // CHUNKS
LAST_CHUNK = 1
LATE_CHUNK = 1
LATE_STEP = -1
AXES = ("outer", "inner")


def features(x):
    x = x.astype(jnp.float32)
    return jnp.where(x > 0.0, x + 1.0, jnp.exp(jnp.minimum(x, 0.0))).astype(jnp.bfloat16)


def head_cols(h):
    return pl.ds(pl.multiple_of(h * HEAD_DIM, HEAD_DIM), HEAD_DIM)


def states_of(half, core, k_ref, v_ref, out_refs):
    for i in range(HALF):
        cols = head_cols((core * HALF + half * HALF + i) % HEADS)
        fk = features(k_ref[:, cols])
        out_refs[i // PER][i % PER] = lax.dot_general(
            fk, v_ref[:, cols], (((0,), (0,)), ((), ())), preferred_element_type=jnp.float32
        )


def theirs_kernel(core_ref, k_hbm, v_hbm, *refs):
    out_refs, (k_ref, v_ref, sems) = refs[:CHUNKS], refs[CHUNKS:]
    copies = [
        pltpu.make_async_copy(k_hbm, k_ref, sems.at[0]),
        pltpu.make_async_copy(v_hbm, v_ref, sems.at[1]),
    ]
    for copy in copies:
        copy.start()
    for copy in copies:
        copy.wait()
    states_of(1, core_ref[0], k_ref, v_ref, out_refs)


def mine_kernel(core_ref, k_ref, v_ref, *out_refs):
    states_of(0, core_ref[0], k_ref, v_ref, out_refs)


def intra_kernel(q_ref, k_ref, v_ref, gain_ref, late_ref, fq_ref, intra_ref, near_gain_ref):
    del late_ref
    near_gain_ref[...] = gain_ref[...]
    rows = q_ref.shape[0]
    causal = lax.broadcasted_iota(jnp.int32, (rows, rows), 0) >= lax.broadcasted_iota(jnp.int32, (rows, rows), 1)
    for h in range(HEADS):
        cols = slice(h * HEAD_DIM, (h + 1) * HEAD_DIM)
        fq = features(q_ref[:, cols])
        fk = features(k_ref[:, cols])
        fq_ref[:, cols] = fq
        scores = lax.dot_general(fq, fk, (((1,), (1,)), ((), ())), preferred_element_type=jnp.float32)
        weights = jnp.where(causal, scores, 0.0).astype(jnp.bfloat16)
        intra_ref[:, cols] = jnp.dot(weights, v_ref[:, cols], preferred_element_type=jnp.float32)


def attend_kernel(jobs, core_ref, fq_ref, intra_ref, gain_ref, *refs):
    carried, (out_hbm, buf_ref, sems) = refs[: len(jobs)], refs[-3:]
    core = core_ref[0]
    copies = []
    for slot, (half, c) in enumerate(jobs):
        first = (core * HALF + half * HALF + c * PER) % HEADS
        for i in range(PER):
            cols = head_cols(first + i)
            state = carried[slot][i].astype(jnp.bfloat16)
            total = intra_ref[:, cols] + jnp.dot(fq_ref[:, cols], state, preferred_element_type=jnp.float32)
            meansq = jnp.mean(total * total, axis=-1, keepdims=True)
            normed = total * lax.rsqrt(meansq + 1e-06) * gain_ref[:, cols]
            buf_ref[slot, :, i * HEAD_DIM : (i + 1) * HEAD_DIM] = normed.astype(jnp.bfloat16)
        width = PER * HEAD_DIM
        place = pl.ds(pl.multiple_of(first * HEAD_DIM, width), width)
        copy = pltpu.make_async_copy(buf_ref.at[slot], out_hbm.at[:, place], sems.at[slot])
        copy.start()
        copies.append(copy)
    for copy in copies:
        copy.wait()


VMEM = pl.BlockSpec(memory_space=pltpu.VMEM)
SMEM = pl.BlockSpec(memory_space=pltpu.SMEM)
HBM = pl.BlockSpec(memory_space=pltpu.HBM)
ANY = pl.BlockSpec(memory_space=pl.ANY)
PARAMS = pltpu.CompilerParams(vmem_limit_bytes=8 * 1024 * 1024)


def levels_of(stride, extent):
    levels = []
    while extent > 1:
        radix = next(r for r in range(2, extent + 1) if extent % r == 0)
        levels.append((stride, radix))
        stride, extent = stride * radix, extent // radix
    return levels


def steps_of(order):
    return [(kind, stride, radix, shift) for kind, (stride, radix) in order for shift in range(1, radix)]


def target(step, i):
    _, stride, radix, shift = step
    digit = i // stride % radix
    return i + ((digit + shift) % radix - digit) * stride


def per_device(outer, inner, queries, keys, values, head_gain):
    rows = queries.shape[0]
    n = outer * inner
    me = lax.axis_index("outer") * inner + lax.axis_index("inner")
    core = me % 2
    even = core == 0
    core_arr = core.reshape(1).astype(jnp.int32)
    f32 = jnp.float32
    part = jax.ShapeDtypeStruct((PER, HEAD_DIM, HEAD_DIM), f32)
    *theirs, near_keys, near_values = pl.pallas_call(
        theirs_kernel,
        out_shape=[part] * CHUNKS + [jax.ShapeDtypeStruct(x.shape, x.dtype) for x in (keys, values)],
        in_specs=[SMEM, HBM, HBM],
        out_specs=[VMEM] * (CHUNKS + 2),
        scratch_shapes=[pltpu.SemaphoreType.DMA((2,))],
        compiler_params=PARAMS,
        name="theirs",
    )(
        core_arr,
        pltpu.with_memory_space_constraint(keys, pltpu.HBM),
        pltpu.with_memory_space_constraint(values, pltpu.HBM),
    )
    mine = pl.pallas_call(
        mine_kernel,
        out_shape=[part] * CHUNKS,
        in_specs=[SMEM, VMEM, VMEM],
        out_specs=[VMEM] * CHUNKS,
        compiler_params=PARAMS,
        cost_estimate=pl.CostEstimate(
            flops=2 * HALF * rows * HEAD_DIM * HEAD_DIM, bytes_accessed=4 * keys.size, transcendentals=keys.size // 2
        ),
        name="mine",
    )(core_arr, near_keys, near_values)

    low = levels_of(2, inner // 2)
    outer_levels = levels_of(inner, outer)
    low, high = low + outer_levels[:1], outer_levels[1:]
    total_low, total_high = [("total", v) for v in low], [("total", v) for v in high]
    prefix_low, prefix_high = [("prefix", v) for v in low[::-1]], [("prefix", v) for v in high[::-1]]
    orders = [(total_high, total_high), (prefix_high, prefix_high)]
    swap = [(i, i ^ 1) for i in range(n)]

    def digit(step):
        return me // step[1] % step[2]

    def to_swap(x):
        return lax.ppermute(x, AXES, swap)

    def scan(evens, odds, before, unit):
        zero, total, entered, sent = jnp.zeros_like(unit), unit, [None, None], []
        for steps in itertools.zip_longest(steps_of(evens), steps_of(odds)):
            messages, kept = [], []
            for q, step in enumerate(steps):
                if step is None:
                    messages.append(zero)
                    kept.append(jnp.bool_(True))
                    continue
                kind, _, radix, shift = step
                if shift == 1:
                    entered[q] = total if kind == "total" else before
                if kind == "total":
                    messages.append(entered[q])
                    kept.append(digit(step) >= shift)
                else:
                    messages.append(entered[q] + jnp.where(digit(step) + shift < radix, unit, zero))
                    kept.append(jnp.bool_(True))
            perm = [(i, target(steps[i % 2], i)) for i in range(n) if steps[i % 2] is not None]
            sent.append(jnp.where(even, messages[0], messages[1]))
            got = lax.ppermute(sent[-1], AXES, perm)
            before = before + jnp.where(jnp.where(even, kept[0], kept[1]), got, zero)
            total = total + got
        return before, total, sent

    partner = [to_swap(x) for x in theirs]
    mine_parts, their_parts = [], []
    late = None
    for c in range(CHUNKS):
        first, second = orders[c % 2]
        zero = jnp.zeros_like(mine[c])
        before, total, _ = scan(total_low, first, zero, mine[c] + partner[c])
        swapped = to_swap(
            jnp.concatenate([jnp.where(even, total, before), mine[c] + jnp.where(even, before, zero)])
        )
        got, more = swapped[:PER], swapped[PER:]
        after, _, sent = scan(
            prefix_low, second, jnp.where(even, got, zero), jnp.where(even, theirs[c] + more, got)
        )
        if c == LATE_CHUNK:
            late = sent[LATE_STEP]
        mine_parts.append(to_swap(after) + jnp.where(even, before, partner[c]))
        their_parts.append(after + jnp.where(even, zero, more))

    fq, intra, gain = pl.pallas_call(
        intra_kernel,
        out_shape=[
            jax.ShapeDtypeStruct(queries.shape, jnp.bfloat16),
            jax.ShapeDtypeStruct(queries.shape, f32),
            jax.ShapeDtypeStruct((1, queries.shape[1]), f32),
        ],
        in_specs=[VMEM] * 4 + [ANY],
        out_specs=[VMEM] * 3,
        compiler_params=PARAMS,
        cost_estimate=pl.CostEstimate(
            flops=4 * HEADS * rows * rows * HEAD_DIM, bytes_accessed=6 * queries.size * 2, transcendentals=queries.size * 2
        ),
        name="intra",
    )(queries, near_keys, near_values, head_gain.reshape(1, -1), late)

    def attend(jobs, parts, so_far=None):
        whole = jax.ShapeDtypeStruct(queries.shape, jnp.bfloat16)
        extra = [] if so_far is None else [so_far]
        given = [core_arr, fq, intra, gain, *parts, *extra]
        return pl.pallas_call(
            functools.partial(attend_kernel, jobs),
            out_shape=whole,
            in_specs=[SMEM] + [VMEM] * (3 + len(jobs)) + [HBM] * len(extra),
            out_specs=HBM,
            scratch_shapes=[
                pltpu.VMEM((len(jobs), rows, PER * HEAD_DIM), jnp.bfloat16),
                pltpu.SemaphoreType.DMA((len(jobs),)),
            ],
            input_output_aliases={len(given) - 1: 0} if extra else {},
            compiler_params=PARAMS,
            cost_estimate=pl.CostEstimate(
                flops=2 * len(jobs) * PER * rows * HEAD_DIM * HEAD_DIM, bytes_accessed=len(jobs) * queries.size, transcendentals=0
            ),
            name="attend",
        )(*given)

    early = [(1, c) for c in range(CHUNKS)] + [(0, c) for c in range(CHUNKS) if c != LAST_CHUNK]
    most = attend(early, their_parts + [x for c, x in enumerate(mine_parts) if c != LAST_CHUNK])
    return attend([(0, LAST_CHUNK)], [mine_parts[LAST_CHUNK]], most)


def solution(mesh):
    outer, inner = mesh.shape["outer"], mesh.shape["inner"]
    assert inner % 2 == 0
    return jax.shard_map(
        functools.partial(per_device, outer, inner),
        mesh=mesh,
        in_specs=(
            P(AXES, None),
            P(AXES, None),
            P(AXES, None),
            P(),
        ),
        out_specs=P(AXES, None),
        check_vma=False,
    )
```

```python
import functools
import itertools

import jax
import jax.numpy as jnp
from jax import lax
from jax.experimental import pallas as pl
from jax.experimental.pallas import tpu as pltpu
from jax.sharding import PartitionSpec as P

HEADS = 8
HEAD_DIM = 128
HALF = HEADS // 2
CHUNKS = 2
PER = HALF // CHUNKS
LAST_CHUNK = 1
LATE_CHUNK = 1
LATE_STEP = -1
AXES = ("outer", "inner")


def features(x):
    x = x.astype(jnp.float32)
    return jnp.where(x > 0.0, x + 1.0, jnp.exp(jnp.minimum(x, 0.0))).astype(jnp.bfloat16)


def head_cols(h):
    return pl.ds(pl.multiple_of(h * HEAD_DIM, HEAD_DIM), HEAD_DIM)


def states_of(half, core, k_ref, v_ref, out_refs):
    for i in range(HALF):
        cols = head_cols((core * HALF + half * HALF + i) % HEADS)
        fk = features(k_ref[:, cols])
        out_refs[i // PER][i % PER] = lax.dot_general(
            fk, v_ref[:, cols], (((0,), (0,)), ((), ())), preferred_element_type=jnp.float32
        )


def theirs_kernel(core_ref, k_hbm, v_hbm, *refs):
    out_refs, (k_ref, v_ref, sems) = refs[:CHUNKS], refs[CHUNKS:]
    copies = [
        pltpu.make_async_copy(k_hbm, k_ref, sems.at[0]),
        pltpu.make_async_copy(v_hbm, v_ref, sems.at[1]),
    ]
    for copy in copies:
        copy.start()
    for copy in copies:
        copy.wait()
    states_of(1, core_ref[0], k_ref, v_ref, out_refs)


def mine_kernel(core_ref, k_ref, v_ref, *out_refs):
    states_of(0, core_ref[0], k_ref, v_ref, out_refs)


def intra_kernel(q_ref, k_ref, v_ref, gain_ref, late_ref, fq_ref, intra_ref, near_gain_ref):
    del late_ref
    near_gain_ref[...] = gain_ref[...]
    rows = q_ref.shape[0]
    causal = lax.broadcasted_iota(jnp.int32, (rows, rows), 0) >= lax.broadcasted_iota(jnp.int32, (rows, rows), 1)
    for h in range(HEADS):
        cols = slice(h * HEAD_DIM, (h + 1) * HEAD_DIM)
        fq = features(q_ref[:, cols])
        fk = features(k_ref[:, cols])
        fq_ref[:, cols] = fq
        scores = lax.dot_general(fq, fk, (((1,), (1,)), ((), ())), preferred_element_type=jnp.float32)
        weights = jnp.where(causal, scores, 0.0).astype(jnp.bfloat16)
        intra_ref[:, cols] = jnp.dot(weights, v_ref[:, cols], preferred_element_type=jnp.float32)


def attend_heads(jobs, core, fq_ref, intra_ref, gain_ref, carried, buf_ref):
    for slot, (half, c) in enumerate(jobs):
        for i in range(PER):
            cols = head_cols((core * HALF + half * HALF + c * PER + i) % HEADS)
            state = carried[slot][i].astype(jnp.bfloat16)
            total = intra_ref[:, cols] + jnp.dot(fq_ref[:, cols], state, preferred_element_type=jnp.float32)
            meansq = jnp.mean(total * total, axis=-1, keepdims=True)
            normed = total * lax.rsqrt(meansq + 1e-06) * gain_ref[:, cols]
            buf_ref[slot, :, i * HEAD_DIM : (i + 1) * HEAD_DIM] = normed.astype(jnp.bfloat16)


def early_kernel(jobs, core_ref, fq_ref, intra_ref, gain_ref, *refs):
    attend_heads(jobs, core_ref[0], fq_ref, intra_ref, gain_ref, refs[:-1], refs[-1])


def last_kernel(jobs, early, core_ref, fq_ref, intra_ref, gain_ref, *refs):
    carried, (early_ref, out_hbm, buf_ref, sems) = refs[: len(jobs)], refs[len(jobs) :]
    core = core_ref[0]
    width = PER * HEAD_DIM

    def copy_out(job, source, sem):
        half, c = job
        first = (core * HALF + half * HALF + c * PER) % HEADS
        place = pl.ds(pl.multiple_of(first * HEAD_DIM, width), width)
        copy = pltpu.make_async_copy(source, out_hbm.at[:, place], sems.at[sem])
        copy.start()
        return copy

    copies = [copy_out(job, early_ref.at[slot], slot) for slot, job in enumerate(early)]
    attend_heads(jobs, core, fq_ref, intra_ref, gain_ref, carried, buf_ref)
    copies += [copy_out(job, buf_ref.at[slot], len(early) + slot) for slot, job in enumerate(jobs)]
    for copy in copies:
        copy.wait()


VMEM = pl.BlockSpec(memory_space=pltpu.VMEM)
SMEM = pl.BlockSpec(memory_space=pltpu.SMEM)
HBM = pl.BlockSpec(memory_space=pltpu.HBM)
ANY = pl.BlockSpec(memory_space=pl.ANY)
PARAMS = pltpu.CompilerParams(vmem_limit_bytes=8 * 1024 * 1024)


def levels_of(stride, extent):
    levels = []
    while extent > 1:
        radix = next(r for r in range(2, extent + 1) if extent % r == 0)
        levels.append((stride, radix))
        stride, extent = stride * radix, extent // radix
    return levels


def steps_of(order):
    return [(kind, stride, radix, shift) for kind, (stride, radix) in order for shift in range(1, radix)]


def target(step, i):
    _, stride, radix, shift = step
    digit = i // stride % radix
    return i + ((digit + shift) % radix - digit) * stride


def per_device(outer, inner, queries, keys, values, head_gain):
    rows = queries.shape[0]
    n = outer * inner
    me = lax.axis_index("outer") * inner + lax.axis_index("inner")
    core = me % 2
    even = core == 0
    core_arr = core.reshape(1).astype(jnp.int32)
    f32 = jnp.float32
    part = jax.ShapeDtypeStruct((PER, HEAD_DIM, HEAD_DIM), f32)
    *theirs, near_keys, near_values = pl.pallas_call(
        theirs_kernel,
        out_shape=[part] * CHUNKS + [jax.ShapeDtypeStruct(x.shape, x.dtype) for x in (keys, values)],
        in_specs=[SMEM, HBM, HBM],
        out_specs=[VMEM] * (CHUNKS + 2),
        scratch_shapes=[pltpu.SemaphoreType.DMA((2,))],
        compiler_params=PARAMS,
        name="theirs",
    )(
        core_arr,
        pltpu.with_memory_space_constraint(keys, pltpu.HBM),
        pltpu.with_memory_space_constraint(values, pltpu.HBM),
    )
    mine = pl.pallas_call(
        mine_kernel,
        out_shape=[part] * CHUNKS,
        in_specs=[SMEM, VMEM, VMEM],
        out_specs=[VMEM] * CHUNKS,
        compiler_params=PARAMS,
        cost_estimate=pl.CostEstimate(
            flops=2 * HALF * rows * HEAD_DIM * HEAD_DIM, bytes_accessed=4 * keys.size, transcendentals=keys.size // 2
        ),
        name="mine",
    )(core_arr, near_keys, near_values)

    low = levels_of(2, inner // 2)
    outer_levels = levels_of(inner, outer)
    low, high = low + outer_levels[:1], outer_levels[1:]
    total_low, total_high = [("total", v) for v in low], [("total", v) for v in high]
    prefix_low, prefix_high = [("prefix", v) for v in low[::-1]], [("prefix", v) for v in high[::-1]]
    orders = [(total_high, total_high), (prefix_high, prefix_high)]
    swap = [(i, i ^ 1) for i in range(n)]

    def digit(step):
        return me // step[1] % step[2]

    def to_swap(x):
        return lax.ppermute(x, AXES, swap)

    def scan(evens, odds, before, unit):
        zero, total, entered, sent = jnp.zeros_like(unit), unit, [None, None], []
        for steps in itertools.zip_longest(steps_of(evens), steps_of(odds)):
            messages, kept = [], []
            for q, step in enumerate(steps):
                if step is None:
                    messages.append(zero)
                    kept.append(jnp.bool_(True))
                    continue
                kind, _, radix, shift = step
                if shift == 1:
                    entered[q] = total if kind == "total" else before
                if kind == "total":
                    messages.append(entered[q])
                    kept.append(digit(step) >= shift)
                else:
                    messages.append(entered[q] + jnp.where(digit(step) + shift < radix, unit, zero))
                    kept.append(jnp.bool_(True))
            perm = [(i, target(steps[i % 2], i)) for i in range(n) if steps[i % 2] is not None]
            sent.append(jnp.where(even, messages[0], messages[1]))
            got = lax.ppermute(sent[-1], AXES, perm)
            before = before + jnp.where(jnp.where(even, kept[0], kept[1]), got, zero)
            total = total + got
        return before, total, sent

    partner = [to_swap(x) for x in theirs]
    mine_parts, their_parts = [], []
    late = None
    for c in range(CHUNKS):
        first, second = orders[c % 2]
        zero = jnp.zeros_like(mine[c])
        before, total, _ = scan(total_low, first, zero, mine[c] + partner[c])
        swapped = to_swap(
            jnp.concatenate([jnp.where(even, total, before), mine[c] + jnp.where(even, before, zero)])
        )
        got, more = swapped[:PER], swapped[PER:]
        after, _, sent = scan(
            prefix_low, second, jnp.where(even, got, zero), jnp.where(even, theirs[c] + more, got)
        )
        if c == LATE_CHUNK:
            late = sent[LATE_STEP]
        mine_parts.append(to_swap(after) + jnp.where(even, before, partner[c]))
        their_parts.append(after + jnp.where(even, zero, more))

    fq, intra, gain = pl.pallas_call(
        intra_kernel,
        out_shape=[
            jax.ShapeDtypeStruct(queries.shape, jnp.bfloat16),
            jax.ShapeDtypeStruct(queries.shape, f32),
            jax.ShapeDtypeStruct((1, queries.shape[1]), f32),
        ],
        in_specs=[VMEM] * 4 + [ANY],
        out_specs=[VMEM] * 3,
        compiler_params=PARAMS,
        cost_estimate=pl.CostEstimate(
            flops=4 * HEADS * rows * rows * HEAD_DIM, bytes_accessed=6 * queries.size * 2, transcendentals=queries.size * 2
        ),
        name="intra",
    )(queries, near_keys, near_values, head_gain.reshape(1, -1), late)

    early = [(1, c) for c in range(CHUNKS)] + [(0, c) for c in range(CHUNKS) if c != LAST_CHUNK]
    jobs = [(0, LAST_CHUNK)]
    early_parts = their_parts + [x for c, x in enumerate(mine_parts) if c != LAST_CHUNK]

    def cost(n_jobs):
        return pl.CostEstimate(
            flops=2 * n_jobs * PER * rows * HEAD_DIM * HEAD_DIM, bytes_accessed=n_jobs * queries.size, transcendentals=0
        )

    done = pl.pallas_call(
        functools.partial(early_kernel, early),
        out_shape=jax.ShapeDtypeStruct((len(early), rows, PER * HEAD_DIM), jnp.bfloat16),
        in_specs=[SMEM] + [VMEM] * (3 + len(early)),
        out_specs=VMEM,
        compiler_params=PARAMS,
        cost_estimate=cost(len(early)),
        name="attend_early",
    )(core_arr, fq, intra, gain, *early_parts)
    return pl.pallas_call(
        functools.partial(last_kernel, jobs, early),
        out_shape=jax.ShapeDtypeStruct(queries.shape, jnp.bfloat16),
        in_specs=[SMEM] + [VMEM] * (3 + len(jobs) + 1),
        out_specs=HBM,
        scratch_shapes=[
            pltpu.VMEM((len(jobs), rows, PER * HEAD_DIM), jnp.bfloat16),
            pltpu.SemaphoreType.DMA((len(early) + len(jobs),)),
        ],
        compiler_params=PARAMS,
        cost_estimate=cost(len(jobs)),
        name="attend_last",
    )(core_arr, fq, intra, gain, mine_parts[LAST_CHUNK], done)


def solution(mesh):
    outer, inner = mesh.shape["outer"], mesh.shape["inner"]
    assert inner % 2 == 0
    return jax.shard_map(
        functools.partial(per_device, outer, inner),
        mesh=mesh,
        in_specs=(
            P(AXES, None),
            P(AXES, None),
            P(AXES, None),
            P(),
        ),
        out_specs=P(AXES, None),
        check_vma=False,
    )
```

```python
import functools
import itertools

import jax
import jax.numpy as jnp
from jax import lax
from jax.experimental import pallas as pl
from jax.experimental.pallas import tpu as pltpu
from jax.sharding import PartitionSpec as P

HEADS = 8
HEAD_DIM = 128
HALF = HEADS // 2
CHUNKS = 2
PER = HALF // CHUNKS
LAST_CHUNK = 1
LATE_CHUNK = 1
LATE_STEP = -1
AXES = ("outer", "inner")


def features(x):
    x = x.astype(jnp.float32)
    return jnp.where(x > 0.0, x + 1.0, jnp.exp(jnp.minimum(x, 0.0))).astype(jnp.bfloat16)


def head_cols(h):
    return pl.ds(pl.multiple_of(h * HEAD_DIM, HEAD_DIM), HEAD_DIM)


def states_of(half, core, k_ref, v_ref, out_refs):
    for i in range(HALF):
        cols = head_cols((core * HALF + half * HALF + i) % HEADS)
        fk = features(k_ref[:, cols])
        out_refs[i // PER][i % PER] = lax.dot_general(
            fk, v_ref[:, cols], (((0,), (0,)), ((), ())), preferred_element_type=jnp.float32
        )


def theirs_kernel(core_ref, k_hbm, v_hbm, *refs):
    out_refs, (k_ref, v_ref, sems) = refs[:CHUNKS], refs[CHUNKS:]
    copies = [
        pltpu.make_async_copy(k_hbm, k_ref, sems.at[0]),
        pltpu.make_async_copy(v_hbm, v_ref, sems.at[1]),
    ]
    for copy in copies:
        copy.start()
    for copy in copies:
        copy.wait()
    states_of(1, core_ref[0], k_ref, v_ref, out_refs)


def mine_kernel(core_ref, k_ref, v_ref, *out_refs):
    states_of(0, core_ref[0], k_ref, v_ref, out_refs)


def intra_kernel(q_ref, k_ref, v_ref, gain_ref, late_ref, fq_ref, intra_ref, near_gain_ref):
    del late_ref
    near_gain_ref[...] = gain_ref[...]
    rows = q_ref.shape[0]
    causal = lax.broadcasted_iota(jnp.int32, (rows, rows), 0) >= lax.broadcasted_iota(jnp.int32, (rows, rows), 1)
    for h in range(HEADS):
        cols = slice(h * HEAD_DIM, (h + 1) * HEAD_DIM)
        fq = features(q_ref[:, cols])
        fk = features(k_ref[:, cols])
        fq_ref[:, cols] = fq
        scores = lax.dot_general(fq, fk, (((1,), (1,)), ((), ())), preferred_element_type=jnp.float32)
        weights = jnp.where(causal, scores, 0.0).astype(jnp.bfloat16)
        intra_ref[:, cols] = jnp.dot(weights, v_ref[:, cols], preferred_element_type=jnp.float32)


def attend_heads(jobs, core, fq_ref, intra_ref, gain_ref, carried, buf_ref):
    for slot, (half, c) in enumerate(jobs):
        for i in range(PER):
            cols = head_cols((core * HALF + half * HALF + c * PER + i) % HEADS)
            state = carried[slot][i].astype(jnp.bfloat16)
            total = intra_ref[:, cols] + jnp.dot(fq_ref[:, cols], state, preferred_element_type=jnp.float32)
            meansq = jnp.mean(total * total, axis=-1, keepdims=True)
            normed = total * lax.rsqrt(meansq + 1e-06) * gain_ref[:, cols]
            buf_ref[slot, :, i * HEAD_DIM : (i + 1) * HEAD_DIM] = normed.astype(jnp.bfloat16)


def early_kernel(jobs, core_ref, fq_ref, intra_ref, gain_ref, *refs):
    attend_heads(jobs, core_ref[0], fq_ref, intra_ref, gain_ref, refs[:-1], refs[-1])


def last_kernel(jobs, early, core_ref, fq_ref, intra_ref, gain_ref, *refs):
    swapped_ref, kept_ref, early_ref, out_hbm, buf_ref, sems = refs
    core = core_ref[0]
    width = PER * HEAD_DIM

    def copy_out(job, source, sem):
        half, c = job
        first = (core * HALF + half * HALF + c * PER) % HEADS
        place = pl.ds(pl.multiple_of(first * HEAD_DIM, width), width)
        copy = pltpu.make_async_copy(source, out_hbm.at[:, place], sems.at[sem])
        copy.start()
        return copy

    copies = [copy_out(job, early_ref.at[slot], slot) for slot, job in enumerate(early)]
    carried = [[swapped_ref[i] + kept_ref[i] for i in range(PER)]]
    attend_heads(jobs, core, fq_ref, intra_ref, gain_ref, carried, buf_ref)
    copies += [copy_out(job, buf_ref.at[slot], len(early) + slot) for slot, job in enumerate(jobs)]
    for copy in copies:
        copy.wait()


VMEM = pl.BlockSpec(memory_space=pltpu.VMEM)
SMEM = pl.BlockSpec(memory_space=pltpu.SMEM)
HBM = pl.BlockSpec(memory_space=pltpu.HBM)
ANY = pl.BlockSpec(memory_space=pl.ANY)
PARAMS = pltpu.CompilerParams(vmem_limit_bytes=8 * 1024 * 1024)


def levels_of(stride, extent):
    levels = []
    while extent > 1:
        radix = next(r for r in range(2, extent + 1) if extent % r == 0)
        levels.append((stride, radix))
        stride, extent = stride * radix, extent // radix
    return levels


def steps_of(order):
    return [(kind, stride, radix, shift) for kind, (stride, radix) in order for shift in range(1, radix)]


def target(step, i):
    _, stride, radix, shift = step
    digit = i // stride % radix
    return i + ((digit + shift) % radix - digit) * stride


def per_device(outer, inner, queries, keys, values, head_gain):
    rows = queries.shape[0]
    n = outer * inner
    me = lax.axis_index("outer") * inner + lax.axis_index("inner")
    core = me % 2
    even = core == 0
    core_arr = core.reshape(1).astype(jnp.int32)
    f32 = jnp.float32
    part = jax.ShapeDtypeStruct((PER, HEAD_DIM, HEAD_DIM), f32)
    *theirs, near_keys, near_values = pl.pallas_call(
        theirs_kernel,
        out_shape=[part] * CHUNKS + [jax.ShapeDtypeStruct(x.shape, x.dtype) for x in (keys, values)],
        in_specs=[SMEM, HBM, HBM],
        out_specs=[VMEM] * (CHUNKS + 2),
        scratch_shapes=[pltpu.SemaphoreType.DMA((2,))],
        compiler_params=PARAMS,
        name="theirs",
    )(
        core_arr,
        pltpu.with_memory_space_constraint(keys, pltpu.HBM),
        pltpu.with_memory_space_constraint(values, pltpu.HBM),
    )
    mine = pl.pallas_call(
        mine_kernel,
        out_shape=[part] * CHUNKS,
        in_specs=[SMEM, VMEM, VMEM],
        out_specs=[VMEM] * CHUNKS,
        compiler_params=PARAMS,
        cost_estimate=pl.CostEstimate(
            flops=2 * HALF * rows * HEAD_DIM * HEAD_DIM, bytes_accessed=4 * keys.size, transcendentals=keys.size // 2
        ),
        name="mine",
    )(core_arr, near_keys, near_values)

    low = levels_of(2, inner // 2)
    outer_levels = levels_of(inner, outer)
    low, high = low + outer_levels[:1], outer_levels[1:]
    total_low, total_high = [("total", v) for v in low], [("total", v) for v in high]
    prefix_low, prefix_high = [("prefix", v) for v in low[::-1]], [("prefix", v) for v in high[::-1]]
    orders = [(total_high, total_high), (prefix_high, prefix_high)]
    swap = [(i, i ^ 1) for i in range(n)]

    def digit(step):
        return me // step[1] % step[2]

    def to_swap(x):
        return lax.ppermute(x, AXES, swap)

    def scan(evens, odds, before, unit):
        zero, total, entered, sent = jnp.zeros_like(unit), unit, [None, None], []
        for steps in itertools.zip_longest(steps_of(evens), steps_of(odds)):
            messages, kept = [], []
            for q, step in enumerate(steps):
                if step is None:
                    messages.append(zero)
                    kept.append(jnp.bool_(True))
                    continue
                kind, _, radix, shift = step
                if shift == 1:
                    entered[q] = total if kind == "total" else before
                if kind == "total":
                    messages.append(entered[q])
                    kept.append(digit(step) >= shift)
                else:
                    messages.append(entered[q] + jnp.where(digit(step) + shift < radix, unit, zero))
                    kept.append(jnp.bool_(True))
            perm = [(i, target(steps[i % 2], i)) for i in range(n) if steps[i % 2] is not None]
            sent.append(jnp.where(even, messages[0], messages[1]))
            got = lax.ppermute(sent[-1], AXES, perm)
            before = before + jnp.where(jnp.where(even, kept[0], kept[1]), got, zero)
            total = total + got
        return before, total, sent

    partner = [to_swap(x) for x in theirs]
    mine_parts, their_parts = [], []
    late = None
    for c in range(CHUNKS):
        first, second = orders[c % 2]
        zero = jnp.zeros_like(mine[c])
        before, total, _ = scan(total_low, first, zero, mine[c] + partner[c])
        swapped = to_swap(
            jnp.concatenate([jnp.where(even, total, before), mine[c] + jnp.where(even, before, zero)])
        )
        got, more = swapped[:PER], swapped[PER:]
        after, _, sent = scan(
            prefix_low, second, jnp.where(even, got, zero), jnp.where(even, theirs[c] + more, got)
        )
        if c == LATE_CHUNK:
            late = sent[LATE_STEP]
        swapped_back, kept_here = to_swap(after), jnp.where(even, before, partner[c])
        if c == LAST_CHUNK:
            last_parts = [swapped_back, kept_here]
        else:
            mine_parts.append(swapped_back + kept_here)
        their_parts.append(after + jnp.where(even, zero, more))

    fq, intra, gain = pl.pallas_call(
        intra_kernel,
        out_shape=[
            jax.ShapeDtypeStruct(queries.shape, jnp.bfloat16),
            jax.ShapeDtypeStruct(queries.shape, f32),
            jax.ShapeDtypeStruct((1, queries.shape[1]), f32),
        ],
        in_specs=[VMEM] * 4 + [ANY],
        out_specs=[VMEM] * 3,
        compiler_params=PARAMS,
        cost_estimate=pl.CostEstimate(
            flops=4 * HEADS * rows * rows * HEAD_DIM, bytes_accessed=6 * queries.size * 2, transcendentals=queries.size * 2
        ),
        name="intra",
    )(queries, near_keys, near_values, head_gain.reshape(1, -1), late)

    early = [(1, c) for c in range(CHUNKS)] + [(0, c) for c in range(CHUNKS) if c != LAST_CHUNK]
    jobs = [(0, LAST_CHUNK)]
    early_parts = their_parts + mine_parts

    def cost(n_jobs):
        return pl.CostEstimate(
            flops=2 * n_jobs * PER * rows * HEAD_DIM * HEAD_DIM, bytes_accessed=n_jobs * queries.size, transcendentals=0
        )

    done = pl.pallas_call(
        functools.partial(early_kernel, early),
        out_shape=jax.ShapeDtypeStruct((len(early), rows, PER * HEAD_DIM), jnp.bfloat16),
        in_specs=[SMEM] + [VMEM] * (3 + len(early)),
        out_specs=VMEM,
        compiler_params=PARAMS,
        cost_estimate=cost(len(early)),
        name="attend_early",
    )(core_arr, fq, intra, gain, *early_parts)
    return pl.pallas_call(
        functools.partial(last_kernel, jobs, early),
        out_shape=jax.ShapeDtypeStruct(queries.shape, jnp.bfloat16),
        in_specs=[SMEM] + [VMEM] * 6,
        out_specs=HBM,
        scratch_shapes=[
            pltpu.VMEM((len(jobs), rows, PER * HEAD_DIM), jnp.bfloat16),
            pltpu.SemaphoreType.DMA((len(early) + len(jobs),)),
        ],
        compiler_params=PARAMS,
        cost_estimate=cost(len(jobs)),
        name="attend_last",
    )(core_arr, fq, intra, gain, *last_parts, done)


def solution(mesh):
    outer, inner = mesh.shape["outer"], mesh.shape["inner"]
    assert inner % 2 == 0
    return jax.shard_map(
        functools.partial(per_device, outer, inner),
        mesh=mesh,
        in_specs=(
            P(AXES, None),
            P(AXES, None),
            P(AXES, None),
            P(),
        ),
        out_specs=P(AXES, None),
        check_vma=False,
    )
```

```python
import functools
import itertools

import jax
import jax.numpy as jnp
from jax import lax
from jax.experimental import pallas as pl
from jax.experimental.pallas import tpu as pltpu
from jax.sharding import PartitionSpec as P

HEADS = 8
HEAD_DIM = 128
HALF = HEADS // 2
CHUNKS = 2
PER = HALF // CHUNKS
LAST_CHUNK = 1
LATE_CHUNK = 1
LATE_STEP = -1
AXES = ("outer", "inner")


def features(x):
    x = x.astype(jnp.float32)
    return jnp.where(x > 0.0, x + 1.0, jnp.exp(jnp.minimum(x, 0.0))).astype(jnp.bfloat16)


def head_cols(h):
    return pl.ds(pl.multiple_of(h * HEAD_DIM, HEAD_DIM), HEAD_DIM)


def states_of(half, core, k_ref, v_ref, out_refs):
    for i in range(HALF):
        cols = head_cols((core * HALF + half * HALF + i) % HEADS)
        fk = features(k_ref[:, cols])
        out_refs[i // PER][i % PER] = lax.dot_general(
            fk, v_ref[:, cols], (((0,), (0,)), ((), ())), preferred_element_type=jnp.float32
        )


def theirs_kernel(core_ref, k_hbm, v_hbm, *refs):
    out_refs, (k_ref, v_ref, sems) = refs[:CHUNKS], refs[CHUNKS:]
    copies = [
        pltpu.make_async_copy(k_hbm, k_ref, sems.at[0]),
        pltpu.make_async_copy(v_hbm, v_ref, sems.at[1]),
    ]
    for copy in copies:
        copy.start()
    for copy in copies:
        copy.wait()
    states_of(1, core_ref[0], k_ref, v_ref, out_refs)


def mine_kernel(core_ref, k_ref, v_ref, *out_refs):
    states_of(0, core_ref[0], k_ref, v_ref, out_refs)


def intra_kernel(q_ref, k_ref, v_ref, gain_ref, late_ref, fq_ref, intra_ref, near_gain_ref):
    del late_ref
    near_gain_ref[...] = gain_ref[...]
    rows = q_ref.shape[0]
    causal = lax.broadcasted_iota(jnp.int32, (rows, rows), 0) >= lax.broadcasted_iota(jnp.int32, (rows, rows), 1)
    for h in range(HEADS):
        cols = slice(h * HEAD_DIM, (h + 1) * HEAD_DIM)
        fq = features(q_ref[:, cols])
        fk = features(k_ref[:, cols])
        fq_ref[:, cols] = fq
        scores = lax.dot_general(fq, fk, (((1,), (1,)), ((), ())), preferred_element_type=jnp.float32)
        weights = jnp.where(causal, scores, 0.0).astype(jnp.bfloat16)
        intra_ref[:, cols] = jnp.dot(weights, v_ref[:, cols], preferred_element_type=jnp.float32)


def attend_heads(jobs, core, fq_ref, intra_ref, gain_ref, carried, buf_ref, finished=None):
    for slot, (half, c) in enumerate(jobs):
        for i in range(PER):
            cols = head_cols((core * HALF + half * HALF + c * PER + i) % HEADS)
            state = carried[slot][i].astype(jnp.bfloat16)
            total = intra_ref[:, cols] + jnp.dot(fq_ref[:, cols], state, preferred_element_type=jnp.float32)
            meansq = jnp.mean(total * total, axis=-1, keepdims=True)
            normed = total * lax.rsqrt(meansq + 1e-06) * gain_ref[:, cols]
            buf_ref[slot, :, i * HEAD_DIM : (i + 1) * HEAD_DIM] = normed.astype(jnp.bfloat16)
            if finished is not None:
                finished(slot, i, cols)


def early_kernel(jobs, core_ref, fq_ref, intra_ref, gain_ref, *refs):
    attend_heads(jobs, core_ref[0], fq_ref, intra_ref, gain_ref, refs[:-1], refs[-1])


def last_kernel(jobs, early, core_ref, fq_ref, intra_ref, gain_ref, *refs):
    carried, (early_ref, out_hbm, buf_ref, sems) = refs[: len(jobs)], refs[len(jobs) :]
    core = core_ref[0]
    width = PER * HEAD_DIM

    def copy_out(job, source, sem):
        half, c = job
        first = (core * HALF + half * HALF + c * PER) % HEADS
        place = pl.ds(pl.multiple_of(first * HEAD_DIM, width), width)
        copy = pltpu.make_async_copy(source, out_hbm.at[:, place], sems.at[sem])
        copy.start()
        return copy

    copies = [copy_out(job, early_ref.at[slot], slot) for slot, job in enumerate(early)]

    def finished(slot, i, cols):
        source = buf_ref.at[slot, :, i * HEAD_DIM : (i + 1) * HEAD_DIM]
        copy = pltpu.make_async_copy(source, out_hbm.at[:, cols], sems.at[len(early) + slot * PER + i])
        copy.start()
        copies.append(copy)

    attend_heads(jobs, core, fq_ref, intra_ref, gain_ref, carried, buf_ref, finished)
    for copy in copies:
        copy.wait()


VMEM = pl.BlockSpec(memory_space=pltpu.VMEM)
SMEM = pl.BlockSpec(memory_space=pltpu.SMEM)
HBM = pl.BlockSpec(memory_space=pltpu.HBM)
ANY = pl.BlockSpec(memory_space=pl.ANY)
PARAMS = pltpu.CompilerParams(vmem_limit_bytes=8 * 1024 * 1024)


def levels_of(stride, extent):
    levels = []
    while extent > 1:
        radix = next(r for r in range(2, extent + 1) if extent % r == 0)
        levels.append((stride, radix))
        stride, extent = stride * radix, extent // radix
    return levels


def steps_of(order):
    return [(kind, stride, radix, shift) for kind, (stride, radix) in order for shift in range(1, radix)]


def target(step, i):
    _, stride, radix, shift = step
    digit = i // stride % radix
    return i + ((digit + shift) % radix - digit) * stride


def per_device(outer, inner, queries, keys, values, head_gain):
    rows = queries.shape[0]
    n = outer * inner
    me = lax.axis_index("outer") * inner + lax.axis_index("inner")
    core = me % 2
    even = core == 0
    core_arr = core.reshape(1).astype(jnp.int32)
    f32 = jnp.float32
    part = jax.ShapeDtypeStruct((PER, HEAD_DIM, HEAD_DIM), f32)
    *theirs, near_keys, near_values = pl.pallas_call(
        theirs_kernel,
        out_shape=[part] * CHUNKS + [jax.ShapeDtypeStruct(x.shape, x.dtype) for x in (keys, values)],
        in_specs=[SMEM, HBM, HBM],
        out_specs=[VMEM] * (CHUNKS + 2),
        scratch_shapes=[pltpu.SemaphoreType.DMA((2,))],
        compiler_params=PARAMS,
        name="theirs",
    )(
        core_arr,
        pltpu.with_memory_space_constraint(keys, pltpu.HBM),
        pltpu.with_memory_space_constraint(values, pltpu.HBM),
    )
    mine = pl.pallas_call(
        mine_kernel,
        out_shape=[part] * CHUNKS,
        in_specs=[SMEM, VMEM, VMEM],
        out_specs=[VMEM] * CHUNKS,
        compiler_params=PARAMS,
        cost_estimate=pl.CostEstimate(
            flops=2 * HALF * rows * HEAD_DIM * HEAD_DIM, bytes_accessed=4 * keys.size, transcendentals=keys.size // 2
        ),
        name="mine",
    )(core_arr, near_keys, near_values)

    low = levels_of(2, inner // 2)
    outer_levels = levels_of(inner, outer)
    low, high = low + outer_levels[:1], outer_levels[1:]
    total_low, total_high = [("total", v) for v in low], [("total", v) for v in high]
    prefix_low, prefix_high = [("prefix", v) for v in low[::-1]], [("prefix", v) for v in high[::-1]]
    orders = [(total_high, total_high), (prefix_high, prefix_high)]
    swap = [(i, i ^ 1) for i in range(n)]

    def digit(step):
        return me // step[1] % step[2]

    def to_swap(x):
        return lax.ppermute(x, AXES, swap)

    def scan(evens, odds, before, unit):
        zero, total, entered, sent = jnp.zeros_like(unit), unit, [None, None], []
        for steps in itertools.zip_longest(steps_of(evens), steps_of(odds)):
            messages, kept = [], []
            for q, step in enumerate(steps):
                if step is None:
                    messages.append(zero)
                    kept.append(jnp.bool_(True))
                    continue
                kind, _, radix, shift = step
                if shift == 1:
                    entered[q] = total if kind == "total" else before
                if kind == "total":
                    messages.append(entered[q])
                    kept.append(digit(step) >= shift)
                else:
                    messages.append(entered[q] + jnp.where(digit(step) + shift < radix, unit, zero))
                    kept.append(jnp.bool_(True))
            perm = [(i, target(steps[i % 2], i)) for i in range(n) if steps[i % 2] is not None]
            sent.append(jnp.where(even, messages[0], messages[1]))
            got = lax.ppermute(sent[-1], AXES, perm)
            before = before + jnp.where(jnp.where(even, kept[0], kept[1]), got, zero)
            total = total + got
        return before, total, sent

    partner = [to_swap(x) for x in theirs]
    mine_parts, their_parts = [], []
    late = None
    for c in range(CHUNKS):
        first, second = orders[c % 2]
        zero = jnp.zeros_like(mine[c])
        before, total, _ = scan(total_low, first, zero, mine[c] + partner[c])
        swapped = to_swap(
            jnp.concatenate([jnp.where(even, total, before), mine[c] + jnp.where(even, before, zero)])
        )
        got, more = swapped[:PER], swapped[PER:]
        after, _, sent = scan(
            prefix_low, second, jnp.where(even, got, zero), jnp.where(even, theirs[c] + more, got)
        )
        if c == LATE_CHUNK:
            late = sent[LATE_STEP]
        mine_parts.append(to_swap(after) + jnp.where(even, before, partner[c]))
        their_parts.append(after + jnp.where(even, zero, more))

    fq, intra, gain = pl.pallas_call(
        intra_kernel,
        out_shape=[
            jax.ShapeDtypeStruct(queries.shape, jnp.bfloat16),
            jax.ShapeDtypeStruct(queries.shape, f32),
            jax.ShapeDtypeStruct((1, queries.shape[1]), f32),
        ],
        in_specs=[VMEM] * 4 + [ANY],
        out_specs=[VMEM] * 3,
        compiler_params=PARAMS,
        cost_estimate=pl.CostEstimate(
            flops=4 * HEADS * rows * rows * HEAD_DIM, bytes_accessed=6 * queries.size * 2, transcendentals=queries.size * 2
        ),
        name="intra",
    )(queries, near_keys, near_values, head_gain.reshape(1, -1), late)

    early = [(1, c) for c in range(CHUNKS)] + [(0, c) for c in range(CHUNKS) if c != LAST_CHUNK]
    jobs = [(0, LAST_CHUNK)]
    early_parts = their_parts + [x for c, x in enumerate(mine_parts) if c != LAST_CHUNK]

    def cost(n_jobs):
        return pl.CostEstimate(
            flops=2 * n_jobs * PER * rows * HEAD_DIM * HEAD_DIM, bytes_accessed=n_jobs * queries.size, transcendentals=0
        )

    done = pl.pallas_call(
        functools.partial(early_kernel, early),
        out_shape=jax.ShapeDtypeStruct((len(early), rows, PER * HEAD_DIM), jnp.bfloat16),
        in_specs=[SMEM] + [VMEM] * (3 + len(early)),
        out_specs=VMEM,
        compiler_params=PARAMS,
        cost_estimate=cost(len(early)),
        name="attend_early",
    )(core_arr, fq, intra, gain, *early_parts)
    return pl.pallas_call(
        functools.partial(last_kernel, jobs, early),
        out_shape=jax.ShapeDtypeStruct(queries.shape, jnp.bfloat16),
        in_specs=[SMEM] + [VMEM] * (3 + len(jobs) + 1),
        out_specs=HBM,
        scratch_shapes=[
            pltpu.VMEM((len(jobs), rows, PER * HEAD_DIM), jnp.bfloat16),
            pltpu.SemaphoreType.DMA((len(early) + len(jobs) * PER,)),
        ],
        compiler_params=PARAMS,
        cost_estimate=cost(len(jobs)),
        name="attend_last",
    )(core_arr, fq, intra, gain, mine_parts[LAST_CHUNK], done)


def solution(mesh):
    outer, inner = mesh.shape["outer"], mesh.shape["inner"]
    assert inner % 2 == 0
    return jax.shard_map(
        functools.partial(per_device, outer, inner),
        mesh=mesh,
        in_specs=(
            P(AXES, None),
            P(AXES, None),
            P(AXES, None),
            P(),
        ),
        out_specs=P(AXES, None),
        check_vma=False,
    )
```

```python
import functools
import itertools

import jax
import jax.numpy as jnp
from jax import lax
from jax.experimental import pallas as pl
from jax.experimental.pallas import tpu as pltpu
from jax.sharding import PartitionSpec as P

HEADS = 8
HEAD_DIM = 128
HALF = HEADS // 2
CHUNKS = 2
PER = HALF // CHUNKS
LAST_CHUNK = 1
LATE_CHUNK = 1
LATE_STEP = -1
AXES = ("outer", "inner")


def features(x):
    x = x.astype(jnp.float32)
    return jnp.where(x > 0.0, x + 1.0, jnp.exp(jnp.minimum(x, 0.0))).astype(jnp.bfloat16)


def head_cols(h):
    return pl.ds(pl.multiple_of(h * HEAD_DIM, HEAD_DIM), HEAD_DIM)


def states_of(half, core, k_ref, v_ref, out_refs):
    for i in range(HALF):
        cols = head_cols((core * HALF + half * HALF + i) % HEADS)
        fk = features(k_ref[:, cols])
        out_refs[i // PER][i % PER] = lax.dot_general(
            fk, v_ref[:, cols], (((0,), (0,)), ((), ())), preferred_element_type=jnp.float32
        )


def theirs_kernel(core_ref, k_hbm, v_hbm, *refs):
    out_refs, (k_ref, v_ref, sems) = refs[:CHUNKS], refs[CHUNKS:]
    copies = [
        pltpu.make_async_copy(k_hbm, k_ref, sems.at[0]),
        pltpu.make_async_copy(v_hbm, v_ref, sems.at[1]),
    ]
    for copy in copies:
        copy.start()
    for copy in copies:
        copy.wait()
    states_of(1, core_ref[0], k_ref, v_ref, out_refs)


def mine_kernel(core_ref, k_ref, v_ref, *out_refs):
    states_of(0, core_ref[0], k_ref, v_ref, out_refs)


def intra_kernel(q_ref, k_ref, v_ref, gain_ref, late_ref, fq_ref, intra_ref, near_gain_ref):
    del late_ref
    near_gain_ref[...] = gain_ref[...]
    rows = q_ref.shape[0]
    causal = lax.broadcasted_iota(jnp.int32, (rows, rows), 0) >= lax.broadcasted_iota(jnp.int32, (rows, rows), 1)
    for h in range(HEADS):
        cols = slice(h * HEAD_DIM, (h + 1) * HEAD_DIM)
        fq = features(q_ref[:, cols])
        fk = features(k_ref[:, cols])
        fq_ref[:, cols] = fq
        scores = lax.dot_general(fq, fk, (((1,), (1,)), ((), ())), preferred_element_type=jnp.float32)
        weights = jnp.where(causal, scores, 0.0).astype(jnp.bfloat16)
        intra_ref[:, cols] = jnp.dot(weights, v_ref[:, cols], preferred_element_type=jnp.float32)


def attend_heads(jobs, core, fq_ref, intra_ref, gain_ref, carried, buf_ref, finished=None):
    work = []
    for slot, (half, c) in enumerate(jobs):
        for i in range(PER):
            cols = head_cols((core * HALF + half * HALF + c * PER + i) % HEADS)
            state = carried[slot][i].astype(jnp.bfloat16)
            total = intra_ref[:, cols] + jnp.dot(fq_ref[:, cols], state, preferred_element_type=jnp.float32)
            work.append((slot, i, cols, total))
    for slot, i, cols, total in work:
        meansq = jnp.mean(total * total, axis=-1, keepdims=True)
        normed = total * lax.rsqrt(meansq + 1e-06) * gain_ref[:, cols]
        buf_ref[slot, :, i * HEAD_DIM : (i + 1) * HEAD_DIM] = normed.astype(jnp.bfloat16)
        if finished is not None:
            finished(slot, i, cols)


def early_kernel(jobs, core_ref, fq_ref, intra_ref, gain_ref, *refs):
    attend_heads(jobs, core_ref[0], fq_ref, intra_ref, gain_ref, refs[:-1], refs[-1])


def last_kernel(jobs, early, core_ref, fq_ref, intra_ref, gain_ref, *refs):
    carried, (early_ref, out_hbm, buf_ref, sems) = refs[: len(jobs)], refs[len(jobs) :]
    core = core_ref[0]
    width = PER * HEAD_DIM

    def copy_out(job, source, sem):
        half, c = job
        first = (core * HALF + half * HALF + c * PER) % HEADS
        place = pl.ds(pl.multiple_of(first * HEAD_DIM, width), width)
        copy = pltpu.make_async_copy(source, out_hbm.at[:, place], sems.at[sem])
        copy.start()
        return copy

    copies = [copy_out(job, early_ref.at[slot], slot) for slot, job in enumerate(early)]

    def finished(slot, i, cols):
        source = buf_ref.at[slot, :, i * HEAD_DIM : (i + 1) * HEAD_DIM]
        copy = pltpu.make_async_copy(source, out_hbm.at[:, cols], sems.at[len(early) + slot * PER + i])
        copy.start()
        copies.append(copy)

    attend_heads(jobs, core, fq_ref, intra_ref, gain_ref, carried, buf_ref, finished)
    for copy in copies:
        copy.wait()


VMEM = pl.BlockSpec(memory_space=pltpu.VMEM)
SMEM = pl.BlockSpec(memory_space=pltpu.SMEM)
HBM = pl.BlockSpec(memory_space=pltpu.HBM)
ANY = pl.BlockSpec(memory_space=pl.ANY)
PARAMS = pltpu.CompilerParams(vmem_limit_bytes=8 * 1024 * 1024)


def levels_of(stride, extent):
    levels = []
    while extent > 1:
        radix = next(r for r in range(2, extent + 1) if extent % r == 0)
        levels.append((stride, radix))
        stride, extent = stride * radix, extent // radix
    return levels


def steps_of(order):
    return [(kind, stride, radix, shift) for kind, (stride, radix) in order for shift in range(1, radix)]


def target(step, i):
    _, stride, radix, shift = step
    digit = i // stride % radix
    return i + ((digit + shift) % radix - digit) * stride


def per_device(outer, inner, queries, keys, values, head_gain):
    rows = queries.shape[0]
    n = outer * inner
    me = lax.axis_index("outer") * inner + lax.axis_index("inner")
    core = me % 2
    even = core == 0
    core_arr = core.reshape(1).astype(jnp.int32)
    f32 = jnp.float32
    part = jax.ShapeDtypeStruct((PER, HEAD_DIM, HEAD_DIM), f32)
    *theirs, near_keys, near_values = pl.pallas_call(
        theirs_kernel,
        out_shape=[part] * CHUNKS + [jax.ShapeDtypeStruct(x.shape, x.dtype) for x in (keys, values)],
        in_specs=[SMEM, HBM, HBM],
        out_specs=[VMEM] * (CHUNKS + 2),
        scratch_shapes=[pltpu.SemaphoreType.DMA((2,))],
        compiler_params=PARAMS,
        name="theirs",
    )(
        core_arr,
        pltpu.with_memory_space_constraint(keys, pltpu.HBM),
        pltpu.with_memory_space_constraint(values, pltpu.HBM),
    )
    mine = pl.pallas_call(
        mine_kernel,
        out_shape=[part] * CHUNKS,
        in_specs=[SMEM, VMEM, VMEM],
        out_specs=[VMEM] * CHUNKS,
        compiler_params=PARAMS,
        cost_estimate=pl.CostEstimate(
            flops=2 * HALF * rows * HEAD_DIM * HEAD_DIM, bytes_accessed=4 * keys.size, transcendentals=keys.size // 2
        ),
        name="mine",
    )(core_arr, near_keys, near_values)

    low = levels_of(2, inner // 2)
    outer_levels = levels_of(inner, outer)
    low, high = low + outer_levels[:1], outer_levels[1:]
    total_low, total_high = [("total", v) for v in low], [("total", v) for v in high]
    prefix_low, prefix_high = [("prefix", v) for v in low[::-1]], [("prefix", v) for v in high[::-1]]
    orders = [(total_high, total_high), (prefix_high, prefix_high)]
    swap = [(i, i ^ 1) for i in range(n)]

    def digit(step):
        return me // step[1] % step[2]

    def to_swap(x):
        return lax.ppermute(x, AXES, swap)

    def scan(evens, odds, before, unit):
        zero, total, entered, sent = jnp.zeros_like(unit), unit, [None, None], []
        for steps in itertools.zip_longest(steps_of(evens), steps_of(odds)):
            messages, kept = [], []
            for q, step in enumerate(steps):
                if step is None:
                    messages.append(zero)
                    kept.append(jnp.bool_(True))
                    continue
                kind, _, radix, shift = step
                if shift == 1:
                    entered[q] = total if kind == "total" else before
                if kind == "total":
                    messages.append(entered[q])
                    kept.append(digit(step) >= shift)
                else:
                    messages.append(entered[q] + jnp.where(digit(step) + shift < radix, unit, zero))
                    kept.append(jnp.bool_(True))
            perm = [(i, target(steps[i % 2], i)) for i in range(n) if steps[i % 2] is not None]
            sent.append(jnp.where(even, messages[0], messages[1]))
            got = lax.ppermute(sent[-1], AXES, perm)
            before = before + jnp.where(jnp.where(even, kept[0], kept[1]), got, zero)
            total = total + got
        return before, total, sent

    partner = [to_swap(x) for x in theirs]
    mine_parts, their_parts = [], []
    late = None
    for c in range(CHUNKS):
        first, second = orders[c % 2]
        zero = jnp.zeros_like(mine[c])
        before, total, _ = scan(total_low, first, zero, mine[c] + partner[c])
        swapped = to_swap(
            jnp.concatenate([jnp.where(even, total, before), mine[c] + jnp.where(even, before, zero)])
        )
        got, more = swapped[:PER], swapped[PER:]
        after, _, sent = scan(
            prefix_low, second, jnp.where(even, got, zero), jnp.where(even, theirs[c] + more, got)
        )
        if c == LATE_CHUNK:
            late = sent[LATE_STEP]
        mine_parts.append(to_swap(after) + jnp.where(even, before, partner[c]))
        their_parts.append(after + jnp.where(even, zero, more))

    fq, intra, gain = pl.pallas_call(
        intra_kernel,
        out_shape=[
            jax.ShapeDtypeStruct(queries.shape, jnp.bfloat16),
            jax.ShapeDtypeStruct(queries.shape, f32),
            jax.ShapeDtypeStruct((1, queries.shape[1]), f32),
        ],
        in_specs=[VMEM] * 4 + [ANY],
        out_specs=[VMEM] * 3,
        compiler_params=PARAMS,
        cost_estimate=pl.CostEstimate(
            flops=4 * HEADS * rows * rows * HEAD_DIM, bytes_accessed=6 * queries.size * 2, transcendentals=queries.size * 2
        ),
        name="intra",
    )(queries, near_keys, near_values, head_gain.reshape(1, -1), late)

    early = [(1, c) for c in range(CHUNKS)] + [(0, c) for c in range(CHUNKS) if c != LAST_CHUNK]
    jobs = [(0, LAST_CHUNK)]
    early_parts = their_parts + [x for c, x in enumerate(mine_parts) if c != LAST_CHUNK]

    def cost(n_jobs):
        return pl.CostEstimate(
            flops=2 * n_jobs * PER * rows * HEAD_DIM * HEAD_DIM, bytes_accessed=n_jobs * queries.size, transcendentals=0
        )

    done = pl.pallas_call(
        functools.partial(early_kernel, early),
        out_shape=jax.ShapeDtypeStruct((len(early), rows, PER * HEAD_DIM), jnp.bfloat16),
        in_specs=[SMEM] + [VMEM] * (3 + len(early)),
        out_specs=VMEM,
        compiler_params=PARAMS,
        cost_estimate=cost(len(early)),
        name="attend_early",
    )(core_arr, fq, intra, gain, *early_parts)
    return pl.pallas_call(
        functools.partial(last_kernel, jobs, early),
        out_shape=jax.ShapeDtypeStruct(queries.shape, jnp.bfloat16),
        in_specs=[SMEM] + [VMEM] * (3 + len(jobs) + 1),
        out_specs=HBM,
        scratch_shapes=[
            pltpu.VMEM((len(jobs), rows, PER * HEAD_DIM), jnp.bfloat16),
            pltpu.SemaphoreType.DMA((len(early) + len(jobs) * PER,)),
        ],
        compiler_params=PARAMS,
        cost_estimate=cost(len(jobs)),
        name="attend_last",
    )(core_arr, fq, intra, gain, mine_parts[LAST_CHUNK], done)


def solution(mesh):
    outer, inner = mesh.shape["outer"], mesh.shape["inner"]
    assert inner % 2 == 0
    return jax.shard_map(
        functools.partial(per_device, outer, inner),
        mesh=mesh,
        in_specs=(
            P(AXES, None),
            P(AXES, None),
            P(AXES, None),
            P(),
        ),
        out_specs=P(AXES, None),
        check_vma=False,
    )
```

```python
import functools
import itertools

import jax
import jax.numpy as jnp
from jax import lax
from jax.experimental import pallas as pl
from jax.experimental.pallas import tpu as pltpu
from jax.sharding import PartitionSpec as P

HEADS = 8
HEAD_DIM = 128
HALF = HEADS // 2
CHUNKS = 2
PER = HALF // CHUNKS
LAST_CHUNK = 1
LATE_CHUNK = 0
LATE_STEP = -1
AXES = ("outer", "inner")


def features(x):
    x = x.astype(jnp.float32)
    return jnp.where(x > 0.0, x + 1.0, jnp.exp(jnp.minimum(x, 0.0))).astype(jnp.bfloat16)


def head_cols(h):
    return pl.ds(pl.multiple_of(h * HEAD_DIM, HEAD_DIM), HEAD_DIM)


def states_of(half, core, k_ref, v_ref, out_refs):
    for i in range(HALF):
        cols = head_cols((core * HALF + half * HALF + i) % HEADS)
        fk = features(k_ref[:, cols])
        out_refs[i // PER][i % PER] = lax.dot_general(
            fk, v_ref[:, cols], (((0,), (0,)), ((), ())), preferred_element_type=jnp.float32
        )


def theirs_kernel(core_ref, k_hbm, v_hbm, *refs):
    out_refs, (k_ref, v_ref, sems) = refs[:CHUNKS], refs[CHUNKS:]
    copies = [
        pltpu.make_async_copy(k_hbm, k_ref, sems.at[0]),
        pltpu.make_async_copy(v_hbm, v_ref, sems.at[1]),
    ]
    for copy in copies:
        copy.start()
    for copy in copies:
        copy.wait()
    states_of(1, core_ref[0], k_ref, v_ref, out_refs)


def mine_kernel(core_ref, k_ref, v_ref, *out_refs):
    states_of(0, core_ref[0], k_ref, v_ref, out_refs)


def intra_kernel(q_ref, k_ref, v_ref, gain_ref, late_ref, fq_ref, intra_ref, near_gain_ref):
    del late_ref
    near_gain_ref[...] = gain_ref[...]
    rows = q_ref.shape[0]
    causal = lax.broadcasted_iota(jnp.int32, (rows, rows), 0) >= lax.broadcasted_iota(jnp.int32, (rows, rows), 1)
    for h in range(HEADS):
        cols = slice(h * HEAD_DIM, (h + 1) * HEAD_DIM)
        fq = features(q_ref[:, cols])
        fk = features(k_ref[:, cols])
        fq_ref[:, cols] = fq
        scores = lax.dot_general(fq, fk, (((1,), (1,)), ((), ())), preferred_element_type=jnp.float32)
        weights = jnp.where(causal, scores, 0.0).astype(jnp.bfloat16)
        intra_ref[:, cols] = jnp.dot(weights, v_ref[:, cols], preferred_element_type=jnp.float32)


def attend_heads(jobs, core, fq_ref, intra_ref, gain_ref, carried, buf_ref, finished=None):
    for slot, (half, c) in enumerate(jobs):
        for i in range(PER):
            cols = head_cols((core * HALF + half * HALF + c * PER + i) % HEADS)
            state = carried[slot][i].astype(jnp.bfloat16)
            total = intra_ref[:, cols] + jnp.dot(fq_ref[:, cols], state, preferred_element_type=jnp.float32)
            meansq = jnp.mean(total * total, axis=-1, keepdims=True)
            normed = total * lax.rsqrt(meansq + 1e-06) * gain_ref[:, cols]
            buf_ref[slot, :, i * HEAD_DIM : (i + 1) * HEAD_DIM] = normed.astype(jnp.bfloat16)
            if finished is not None:
                finished(slot, i, cols)


def early_kernel(jobs, core_ref, fq_ref, intra_ref, gain_ref, *refs):
    attend_heads(jobs, core_ref[0], fq_ref, intra_ref, gain_ref, refs[:-1], refs[-1])


def last_kernel(jobs, early, core_ref, fq_ref, intra_ref, gain_ref, *refs):
    carried, (early_ref, out_hbm, buf_ref, sems) = refs[: len(jobs)], refs[len(jobs) :]
    core = core_ref[0]
    width = PER * HEAD_DIM

    def copy_out(job, source, sem):
        half, c = job
        first = (core * HALF + half * HALF + c * PER) % HEADS
        place = pl.ds(pl.multiple_of(first * HEAD_DIM, width), width)
        copy = pltpu.make_async_copy(source, out_hbm.at[:, place], sems.at[sem])
        copy.start()
        return copy

    copies = [copy_out(job, early_ref.at[slot], slot) for slot, job in enumerate(early)]

    def finished(slot, i, cols):
        source = buf_ref.at[slot, :, i * HEAD_DIM : (i + 1) * HEAD_DIM]
        copy = pltpu.make_async_copy(source, out_hbm.at[:, cols], sems.at[len(early) + slot * PER + i])
        copy.start()
        copies.append(copy)

    attend_heads(jobs, core, fq_ref, intra_ref, gain_ref, carried, buf_ref, finished)
    for copy in copies:
        copy.wait()


VMEM = pl.BlockSpec(memory_space=pltpu.VMEM)
SMEM = pl.BlockSpec(memory_space=pltpu.SMEM)
HBM = pl.BlockSpec(memory_space=pltpu.HBM)
ANY = pl.BlockSpec(memory_space=pl.ANY)
PARAMS = pltpu.CompilerParams(vmem_limit_bytes=8 * 1024 * 1024)


def levels_of(stride, extent):
    levels = []
    while extent > 1:
        radix = next(r for r in range(2, extent + 1) if extent % r == 0)
        levels.append((stride, radix))
        stride, extent = stride * radix, extent // radix
    return levels


def steps_of(order):
    return [(kind, stride, radix, shift) for kind, (stride, radix) in order for shift in range(1, radix)]


def target(step, i):
    _, stride, radix, shift = step
    digit = i // stride % radix
    return i + ((digit + shift) % radix - digit) * stride


def per_device(outer, inner, queries, keys, values, head_gain):
    rows = queries.shape[0]
    n = outer * inner
    me = lax.axis_index("outer") * inner + lax.axis_index("inner")
    core = me % 2
    even = core == 0
    core_arr = core.reshape(1).astype(jnp.int32)
    f32 = jnp.float32
    part = jax.ShapeDtypeStruct((PER, HEAD_DIM, HEAD_DIM), f32)
    *theirs, near_keys, near_values = pl.pallas_call(
        theirs_kernel,
        out_shape=[part] * CHUNKS + [jax.ShapeDtypeStruct(x.shape, x.dtype) for x in (keys, values)],
        in_specs=[SMEM, HBM, HBM],
        out_specs=[VMEM] * (CHUNKS + 2),
        scratch_shapes=[pltpu.SemaphoreType.DMA((2,))],
        compiler_params=PARAMS,
        name="theirs",
    )(
        core_arr,
        pltpu.with_memory_space_constraint(keys, pltpu.HBM),
        pltpu.with_memory_space_constraint(values, pltpu.HBM),
    )
    mine = pl.pallas_call(
        mine_kernel,
        out_shape=[part] * CHUNKS,
        in_specs=[SMEM, VMEM, VMEM],
        out_specs=[VMEM] * CHUNKS,
        compiler_params=PARAMS,
        cost_estimate=pl.CostEstimate(
            flops=2 * HALF * rows * HEAD_DIM * HEAD_DIM, bytes_accessed=4 * keys.size, transcendentals=keys.size // 2
        ),
        name="mine",
    )(core_arr, near_keys, near_values)

    low = levels_of(2, inner // 2)
    outer_levels = levels_of(inner, outer)
    low, high = low + outer_levels[:1], outer_levels[1:]
    total_low, total_high = [("total", v) for v in low], [("total", v) for v in high]
    prefix_low, prefix_high = [("prefix", v) for v in low[::-1]], [("prefix", v) for v in high[::-1]]
    orders = [(total_high, total_high), (prefix_high, prefix_high)]
    swap = [(i, i ^ 1) for i in range(n)]

    def digit(step):
        return me // step[1] % step[2]

    def to_swap(x):
        return lax.ppermute(x, AXES, swap)

    def scan(evens, odds, before, unit):
        zero, total, entered, sent = jnp.zeros_like(unit), unit, [None, None], []
        for steps in itertools.zip_longest(steps_of(evens), steps_of(odds)):
            messages, kept = [], []
            for q, step in enumerate(steps):
                if step is None:
                    messages.append(zero)
                    kept.append(jnp.bool_(True))
                    continue
                kind, _, radix, shift = step
                if shift == 1:
                    entered[q] = total if kind == "total" else before
                if kind == "total":
                    messages.append(entered[q])
                    kept.append(digit(step) >= shift)
                else:
                    messages.append(entered[q] + jnp.where(digit(step) + shift < radix, unit, zero))
                    kept.append(jnp.bool_(True))
            perm = [(i, target(steps[i % 2], i)) for i in range(n) if steps[i % 2] is not None]
            sent.append(jnp.where(even, messages[0], messages[1]))
            got = lax.ppermute(sent[-1], AXES, perm)
            before = before + jnp.where(jnp.where(even, kept[0], kept[1]), got, zero)
            total = total + got
        return before, total, sent

    partner = [to_swap(x) for x in theirs]
    mine_parts, their_parts = [], []
    late = None
    for c in range(CHUNKS):
        first, second = orders[c % 2]
        zero = jnp.zeros_like(mine[c])
        before, total, _ = scan(total_low, first, zero, mine[c] + partner[c])
        swapped = to_swap(
            jnp.concatenate([jnp.where(even, total, before), mine[c] + jnp.where(even, before, zero)])
        )
        got, more = swapped[:PER], swapped[PER:]
        after, _, sent = scan(
            prefix_low, second, jnp.where(even, got, zero), jnp.where(even, theirs[c] + more, got)
        )
        if c == LATE_CHUNK:
            late = sent[LATE_STEP]
        mine_parts.append(to_swap(after) + jnp.where(even, before, partner[c]))
        their_parts.append(after + jnp.where(even, zero, more))

    fq, intra, gain = pl.pallas_call(
        intra_kernel,
        out_shape=[
            jax.ShapeDtypeStruct(queries.shape, jnp.bfloat16),
            jax.ShapeDtypeStruct(queries.shape, f32),
            jax.ShapeDtypeStruct((1, queries.shape[1]), f32),
        ],
        in_specs=[VMEM] * 4 + [ANY],
        out_specs=[VMEM] * 3,
        compiler_params=PARAMS,
        cost_estimate=pl.CostEstimate(
            flops=4 * HEADS * rows * rows * HEAD_DIM, bytes_accessed=6 * queries.size * 2, transcendentals=queries.size * 2
        ),
        name="intra",
    )(queries, near_keys, near_values, head_gain.reshape(1, -1), late)

    early = [(1, c) for c in range(CHUNKS)] + [(0, c) for c in range(CHUNKS) if c != LAST_CHUNK]
    jobs = [(0, LAST_CHUNK)]
    early_parts = their_parts + [x for c, x in enumerate(mine_parts) if c != LAST_CHUNK]

    def cost(n_jobs):
        return pl.CostEstimate(
            flops=2 * n_jobs * PER * rows * HEAD_DIM * HEAD_DIM, bytes_accessed=n_jobs * queries.size, transcendentals=0
        )

    done = pl.pallas_call(
        functools.partial(early_kernel, early),
        out_shape=jax.ShapeDtypeStruct((len(early), rows, PER * HEAD_DIM), jnp.bfloat16),
        in_specs=[SMEM] + [VMEM] * (3 + len(early)),
        out_specs=VMEM,
        compiler_params=PARAMS,
        cost_estimate=cost(len(early)),
        name="attend_early",
    )(core_arr, fq, intra, gain, *early_parts)
    return pl.pallas_call(
        functools.partial(last_kernel, jobs, early),
        out_shape=jax.ShapeDtypeStruct(queries.shape, jnp.bfloat16),
        in_specs=[SMEM] + [VMEM] * (3 + len(jobs) + 1),
        out_specs=HBM,
        scratch_shapes=[
            pltpu.VMEM((len(jobs), rows, PER * HEAD_DIM), jnp.bfloat16),
            pltpu.SemaphoreType.DMA((len(early) + len(jobs) * PER,)),
        ],
        compiler_params=PARAMS,
        cost_estimate=cost(len(jobs)),
        name="attend_last",
    )(core_arr, fq, intra, gain, mine_parts[LAST_CHUNK], done)


def solution(mesh):
    outer, inner = mesh.shape["outer"], mesh.shape["inner"]
    assert inner % 2 == 0
    return jax.shard_map(
        functools.partial(per_device, outer, inner),
        mesh=mesh,
        in_specs=(
            P(AXES, None),
            P(AXES, None),
            P(AXES, None),
            P(),
        ),
        out_specs=P(AXES, None),
        check_vma=False,
    )
```
